512 devices in a mesh: tensor: 32 (over z, y_lo), dp: 16 (over y_hi, x, core).
Axes of the slice: x: 4, y: 4 (y_hi: 2, y_lo: 2; y = y_hi * 2 + y_lo), z: 16, core: 2. Of those that a mesh axis runs over, the one named last changes fastest.
Arguments:
- stream: bfloat16 [512, 12288], P('tensor', 'dp'), may hold values from -150 to 150
- norm_gain: float32 [12288], P('dp'), may hold values from 0.1 to 1.9
- head_weight: bfloat16 [16384, 12288], P('tensor', 'dp'), may hold values from -1 to 1
- down_weight: bfloat16 [14336, 12288], P('tensor', 'dp'), may hold values from -0.046875 to 0.046875
- gate_pre: bfloat16 [512, 14336], P('dp', 'tensor'), may hold values from -6 to 6
- up_pre: bfloat16 [512, 14336], P('dp', 'tensor'), may hold values from -6 to 6
- targets: int32 [512], P('dp'), may hold values from 0 to 16383
- token_weight: float32 [512], P('dp'), may hold values from 1 to 120
Outputs:
- head_grad: float32 [16384, 12288], P('tensor', 'dp')
- down_grad: float32 [14336, 12288], P('tensor', 'dp')
- stream_grad: bfloat16 [512, 12288], P('tensor', 'dp')
- gain_grad: float32 [12288], P('dp')
- gate_grad: bfloat16 [512, 14336], P('dp', 'tensor')
- up_grad: bfloat16 [512, 14336], P('dp', 'tensor')
The draws below stay inside these ranges and needn't reach their ends.
All inputs are finite; a program needn't handle non-finite values.
Results may differ from the reference program's by a relative error of at most 0.02.
Values may be sent and summed in bfloat16 or wider, within the bound.
No kernel may reach another device: no remote copies, remote signals or barrier semaphores. Data moves between devices by JAX's collectives and lax.ppermute only.
A program may use at most 64 MiB of HBM per device.

```python
import math
import jax
import jax.numpy as jnp
import numpy as np
from jax import lax

D = 12288
V_DEV = 512
V = 16384
FF = 14336
TOKENS = 512
N_TENSOR = 32


def draw_stream(key, part):
    key = jax.random.fold_in(key, 1)
    row_key, col_key, value_key = jax.random.split(key, 3)
    row_scale = jnp.exp(jax.random.uniform(row_key, (TOKENS, 1), jnp.float32) * math.log(10.0))
    col_scale = jnp.exp(jax.random.uniform(col_key, (1, D), jnp.float32) * math.log(10.0))
    values = jax.random.normal(value_key, (TOKENS, D), jnp.float32)
    field = values * row_scale * col_scale / 4.0
    return jnp.clip(field, -150.0, 150.0).astype(jnp.bfloat16)


def draw_head_weight(key, part):
    key = jax.random.fold_in(key, 2)
    spread = 3.0 / math.sqrt(D)
    vocab_size = V_DEV * N_TENSOR
    field = jnp.clip(jax.random.normal(key, (vocab_size, D), jnp.float32), -6.0, 6.0) * spread
    return field.astype(jnp.bfloat16)


def draw_token_weight(key, part):
    key = jax.random.fold_in(key, 3)
    position = jnp.arange(TOKENS, dtype=jnp.float32) / TOKENS
    factor = jnp.exp(jax.random.uniform(key, (TOKENS,), jnp.float32) * math.log(4.0))
    trend = 2.0 * jnp.exp(position * math.log(10.0))
    return trend * factor


def touch_ends(entries, own_key, smallest, high):
    longest = entries.shape.index(max(entries.shape))
    spots = []
    for shift in (0, 1):
        where = [jax.random.randint(jax.random.fold_in(own_key, axis), (), 0, length) for axis, length in enumerate(entries.shape)]
        where[longest] = (where[longest] + shift) % entries.shape[longest]
        spots.append(tuple(where))
    return entries.at[spots[0]].set(smallest).at[spots[1]].set(high)


def block_levels(stream_key, extent, pieces, smallest, largest):
    factor_of, own = 1.0, jax.random.fold_in(stream_key, 6)
    for dim, shards_of in pieces:
        heights = jnp.exp(jax.random.uniform(jax.random.fold_in(own, dim), (shards_of,), jnp.float32, smallest / len(pieces), largest / len(pieces)))
        factor_of = factor_of * jnp.repeat(heights, extent[dim] // shards_of).reshape([-1 if axis == dim else 1 for axis in range(len(extent))])
    return factor_of


def cumulative_ranks(amount, lean):
    weights = [(1 << 20) // math.isqrt(grade ** lean) + 1 for grade in range(1, amount + 1)]
    width = 1 + sum(weights) // (1 << 30)
    return np.cumsum(np.array([max(1, weight // width) for weight in weights]))


def skewed_ids(rng, shape, amount, lean):
    table = cumulative_ranks(amount, lean)
    lot = jax.random.randint(jax.random.fold_in(rng, 1), shape, 0, int(table[amount - 1]))
    standing = jnp.searchsorted(jnp.asarray(table, jnp.int32), lot, side="right")
    return jax.random.permutation(jax.random.fold_in(rng, 2), amount)[standing].astype(jnp.int32)


def centred(key, extent, deviation, reach, cuts=(), kind=jnp.bfloat16):
    values = jax.random.normal(key, extent, jnp.float32) * deviation
    if len(cuts) > 0:
        values = block_levels(key, extent, cuts, -0.22, 0.18) * values
    return jnp.clip(values, min=-reach, max=reach).astype(kind)


def setup_inputs(seed: int = 0) -> dict:
    streams_of = jax.random.split(jax.random.key(seed), 9)
    stream = draw_stream(jax.random.fold_in(streams_of[8], 71), 0)
    norm_gain = jnp.clip(1.0 + 0.18 * jax.random.normal(streams_of[1], (D,), jnp.float32), 0.1, 1.9)
    head_weight = draw_head_weight(jax.random.fold_in(streams_of[8], 71), 0)
    down_weight = centred(streams_of[3], (FF, D), FF ** -0.5, 0.046875, ((0, 32), (1, 16)))
    gate_pre = centred(streams_of[4], (TOKENS, FF), 1.0, 6.0, ((0, 16), (1, 32)))
    up_pre = centred(streams_of[5], (TOKENS, FF), 1.0, 6.0, ((0, 16), (1, 32)))
    targets = touch_ends(skewed_ids(streams_of[6], (TOKENS,), V, 2), jax.random.fold_in(streams_of[6], 3), 0, V - 1).astype(jnp.int32)
    token_weight = draw_token_weight(jax.random.fold_in(streams_of[8], 71), 0)
    return {"stream": stream, "norm_gain": norm_gain, "head_weight": head_weight, "down_weight": down_weight, "gate_pre": gate_pre, "up_pre": up_pre, "targets": targets, "token_weight": token_weight}


epsilon = 1e-05

def reference(stream, norm_gain, head_weight, down_weight, gate_pre, up_pre, targets, token_weight):
    vocab_size = V_DEV * N_TENSOR
    stream_float = stream.astype(jnp.float32)
    inv_rms = lax.rsqrt(lax.optimization_barrier(jnp.sum(stream_float * stream_float, axis=1)) / D + epsilon)
    unit_rows = stream_float * inv_rms[:, None]
    normed = (unit_rows * norm_gain).astype(jnp.bfloat16)
    logits = jnp.dot(normed, head_weight.T, preferred_element_type=jnp.float32)
    row_top = lax.optimization_barrier(jnp.max(logits, axis=1, keepdims=True))
    shifted = jnp.exp(logits - row_top)
    probability = shifted / lax.optimization_barrier(jnp.sum(shifted, axis=1, keepdims=True))
    matches = (targets[:, None] == jnp.arange(vocab_size, dtype=jnp.int32)[None, :]).astype(jnp.float32)
    dlogits = ((probability - matches) * token_weight[:, None]).astype(jnp.bfloat16)
    head_grad = jnp.dot(dlogits.T, normed, preferred_element_type=jnp.float32)
    normed_grad = jnp.dot(dlogits, head_weight, preferred_element_type=jnp.float32)
    gain_grad = lax.optimization_barrier(jnp.sum(normed_grad * unit_rows, axis=0))
    scaled = normed_grad * norm_gain
    inner_sums = lax.optimization_barrier(jnp.sum(scaled * unit_rows, axis=1)) / D
    stream_grad = (inv_rms[:, None] * (scaled - unit_rows * inner_sums[:, None])).astype(jnp.bfloat16)
    hidden_grad = jnp.dot(stream_grad, down_weight.T, preferred_element_type=jnp.float32)
    gate_float = gate_pre.astype(jnp.float32)
    up_float = up_pre.astype(jnp.float32)
    sigmoid_gate = jax.nn.sigmoid(gate_float)
    hidden = (gate_float * sigmoid_gate * up_float).astype(jnp.bfloat16)
    down_grad = jnp.dot(hidden.T, stream_grad, preferred_element_type=jnp.float32)
    up_grad = (hidden_grad * gate_float * sigmoid_gate).astype(jnp.bfloat16)
    gate_grad = (hidden_grad * up_float * sigmoid_gate * (1.0 + gate_float * (1.0 - sigmoid_gate))).astype(jnp.bfloat16)
    return (head_grad, down_grad, stream_grad, gain_grad, gate_grad, up_grad)
```

```python
import jax
import jax.numpy as jnp
from jax import lax
from jax.sharding import Mesh, PartitionSpec as P

D = 12288
EPSILON = 1e-05
FAR, NEAR = ("za",), ("zb", "yl")
TENSOR = FAR + NEAR
DP = ("yh", "x", "c")
f32, bf16 = jnp.float32, jnp.bfloat16


def exchange(blocks, axes):
    return lax.all_to_all(blocks, axes, 0, 0, tiled=True)


def spread(block, axes, n):
    return exchange(jnp.broadcast_to(block[None], (n,) + block.shape), axes)


def gather_tensor(block):
    far = spread(block, FAR, 4)
    near = spread(far, NEAR, 8)
    return near.transpose(1, 0, 2, 3).reshape(32 * block.shape[0], block.shape[1])


def scatter_tensor(partial):
    rows, columns = partial.shape[0] // 32, partial.shape[1]
    near = exchange(
        partial.reshape(4, 8, rows, columns).transpose(1, 0, 2, 3).astype(bf16), NEAR
    )
    near = jnp.sum(near.astype(f32), axis=0).astype(bf16)
    far = exchange(near, FAR)
    return jnp.sum(far.astype(f32), axis=0)


def split3(v):
    hi = lax.reduce_precision(v, 8, 7)
    mid = lax.reduce_precision(v - hi, 8, 7)
    lo = lax.reduce_precision(v - hi - mid, 8, 7)
    return jnp.stack([hi, mid, lo], axis=-1).astype(bf16)


def join3(s):
    s = s.astype(f32)
    return s[..., 0] + s[..., 1] + s[..., 2]


def gather_and_sum(block, term):
    def join_rows(rows, row):
        extra = jnp.pad(split3(row).T, ((0, 5), (0, 0)))
        return jnp.concatenate([rows, extra], axis=0)

    def sum_rows(got, at):
        extra = got[:, at : at + 3].astype(f32)
        return jnp.sum(extra, axis=(0, 1))

    n = block.shape[0]
    far = spread(join_rows(block, term), FAR, 4)
    term = sum_rows(far, n)
    near = spread(join_rows(far[:, :n].reshape(4 * n, -1), term), NEAR, 8)
    term = sum_rows(near, 4 * n)
    near = near[:, : 4 * n].reshape(8, 4, n, -1)
    return near.transpose(1, 0, 2, 3).reshape(32 * n, -1), term


def per_device(
    stream, norm_gain, head_weight, down_weight, gate_pre, up_pre, targets, token_weight
):
    vocab_local = head_weight.shape[0]
    t = lax.axis_index(TENSOR)
    x_all = gather_tensor(stream).astype(f32)
    xg = (x_all * norm_gain).astype(bf16)
    squares = jnp.sum(x_all * x_all, axis=1)
    part = jnp.einsum("td,vd->tv", xg, head_weight, preferred_element_type=f32).astype(bf16)
    sq = jnp.pad(split3(squares), ((0, 0), (0, 125)))
    got = exchange(jnp.concatenate([part, sq], axis=1).reshape(16, 32, 640), DP)
    got = jnp.sum(got.astype(f32), axis=0)
    inv = lax.rsqrt((got[:, 512] + got[:, 513] + got[:, 514]) / D + EPSILON)
    logits = got[:, :512] * inv[:, None]
    top = jnp.max(logits, axis=1)
    e = jnp.exp(logits - top[:, None])
    columns = t * vocab_local + lax.iota(jnp.int32, vocab_local)
    matches = targets[:, None] == columns[None, :]
    stats = jnp.stack(
        [
            top,
            jnp.sum(e, axis=1),
            jnp.sum(e * logits, axis=1),
            jnp.sum(jnp.where(matches, logits, 0.0), axis=1),
        ]
    ).reshape(1, 128)
    stats = spread(stats, TENSOR, 32).reshape(32, 4, 32)
    tops = stats[:, 0]
    global_top = jnp.max(tops, axis=0)
    scale = jnp.exp(tops - global_top)
    total = jnp.sum(stats[:, 1] * scale, axis=0)
    mean = jnp.sum(stats[:, 2] * scale, axis=0) / total
    inner = token_weight * (mean - jnp.sum(stats[:, 3], axis=0)) / D
    here = jnp.exp(logits - global_top[:, None]) / total[:, None]
    dlogits = ((here - matches.astype(f32)) * token_weight[:, None]).astype(bf16)
    gate_float = gate_pre.astype(f32)
    up_float = up_pre.astype(f32)
    sigmoid_gate = jax.nn.sigmoid(gate_float)
    hidden = (gate_float * sigmoid_gate * up_float).astype(bf16)
    scalars = jnp.pad(
        jnp.concatenate([split3(inv), split3(inner)], axis=1), ((0, 0), (0, 58))
    )
    sent = jnp.concatenate([dlogits, hidden, scalars], axis=1)
    got = spread(sent, DP, 16).reshape(512, 1024)
    piece = got[:, :512]
    hidden_all = got[:, 512:960]
    inv_all = join3(got[:, 960:963])
    inner_all = join3(got[:, 963:966])
    normed_all = (x_all * inv_all[:, None] * norm_gain).astype(bf16)
    weight_part = jnp.einsum("tv,td->vd", piece, normed_all, preferred_element_type=f32)
    back_rows = jnp.dot(piece, head_weight, preferred_element_type=f32)
    normed_back = scatter_tensor(back_rows)
    inv_own = lax.dynamic_slice_in_dim(inv_all, t * 16, 16)[:, None]
    inner_own = lax.dynamic_slice_in_dim(inner_all, t * 16, 16)[:, None]
    unit_rows = stream.astype(f32) * inv_own
    stream_grad = (inv_own * (normed_back * norm_gain - unit_rows * inner_own)).astype(bf16)
    gain_part = jnp.sum(normed_back * unit_rows, axis=0)
    stream_all, gain_grad = gather_and_sum(stream_grad, gain_part)
    hidden_part = jnp.einsum(
        "td,fd->tf", stream_all, down_weight, preferred_element_type=f32
    ).astype(bf16)
    hidden_back = jnp.sum(exchange(hidden_part.reshape(16, 32, 448), DP).astype(f32), axis=0)
    down_grad = jnp.einsum("tf,td->fd", hidden_all, stream_all, preferred_element_type=f32)
    up_grad = (hidden_back * gate_float * sigmoid_gate).astype(bf16)
    gate_grad = (
        hidden_back * up_float * sigmoid_gate * (1.0 + gate_float * (1.0 - sigmoid_gate))
    ).astype(bf16)
    return (weight_part, down_grad, stream_grad, gain_grad, gate_grad, up_grad)


def solution(mesh):
    fine = Mesh(mesh.devices.reshape(4, 4, 2, 2, 4, 2), ("za", "zb", "yl", "yh", "x", "c"))
    return jax.shard_map(
        per_device,
        mesh=fine,
        in_specs=(
            P(TENSOR, DP),
            P(DP),
            P(TENSOR, DP),
            P(TENSOR, DP),
            P(DP, TENSOR),
            P(DP, TENSOR),
            P(DP),
            P(DP),
        ),
        out_specs=(
            P(TENSOR, DP),
            P(TENSOR, DP),
            P(TENSOR, DP),
            P(DP),
            P(DP, TENSOR),
            P(DP, TENSOR),
        ),
        check_vma=False,
    )
```

```python
import jax
import jax.numpy as jnp
from jax import lax
from jax.sharding import Mesh, PartitionSpec as P

D = 12288
EPSILON = 1e-05
FAR, NEAR = ("zf",), ("zn", "yl")
TENSOR = FAR + NEAR
DP = ("yh", "x", "c")
FARS, NEARS = 8, 4
f32, bf16 = jnp.float32, jnp.bfloat16


def exchange(blocks, axes):
    return lax.all_to_all(blocks, axes, 0, 0, tiled=True)


def spread(block, axes, n):
    return exchange(jnp.broadcast_to(block[None], (n,) + block.shape), axes)


def gather_tensor(block):
    return spread(spread(block, FAR, FARS), NEAR, NEARS)


def in_order(blocks):
    return blocks.transpose(1, 0, 2, 3).reshape(-1, blocks.shape[-1])


def scatter_tensor(partial):
    rows, columns = partial.shape[0] // 32, partial.shape[1]
    near = exchange(partial.reshape(NEARS, FARS, rows, columns).astype(bf16), NEAR)
    near = jnp.sum(near.astype(f32), axis=0).astype(bf16)
    far = exchange(near, FAR)
    return jnp.sum(far.astype(f32), axis=0)


def split3(v):
    hi = lax.reduce_precision(v, 8, 7)
    mid = lax.reduce_precision(v - hi, 8, 7)
    lo = lax.reduce_precision(v - hi - mid, 8, 7)
    return jnp.stack([hi, mid, lo], axis=-1).astype(bf16)


def join3(s):
    s = s.astype(f32)
    return s[..., 0] + s[..., 1] + s[..., 2]


def gather_and_sum(block, term):
    n, columns = block.shape
    pair = split3(term)[:, :2].T.reshape(2 * columns // 128, 128)
    side = jnp.pad(pair, ((0, n - pair.shape[0]), (0, 0)))
    far = spread(jnp.concatenate([block, side], axis=1), FAR, FARS)
    side = far[:, : pair.shape[0], columns:].astype(f32).reshape(FARS, 2, columns)
    term = jnp.sum(side, axis=(0, 1))
    rows = far[:, :, :columns].reshape(FARS * n, columns)
    extra = jnp.pad(split3(term).T, ((0, 5), (0, 0)))
    near = spread(jnp.concatenate([rows, extra], axis=0), NEAR, NEARS)
    term = jnp.sum(near[:, FARS * n : FARS * n + 3].astype(f32), axis=(0, 1))
    return near[:, : FARS * n].reshape(NEARS, FARS, n, columns), term


def per_device(
    stream, norm_gain, head_weight, down_weight, gate_pre, up_pre, targets, token_weight
):
    vocab_local = head_weight.shape[0]
    t = lax.axis_index(TENSOR)
    x_all = in_order(gather_tensor(stream)).astype(f32)
    xg = lax.optimization_barrier((x_all * norm_gain).astype(bf16))
    squares = jnp.sum(x_all * x_all, axis=1)
    part = jnp.einsum("td,vd->tv", xg, head_weight, preferred_element_type=f32).astype(bf16)
    sq = jnp.pad(split3(squares), ((0, 0), (0, 125)))
    got = exchange(jnp.concatenate([part, sq], axis=1).reshape(16, 32, 640), DP)
    got = jnp.sum(got.astype(f32), axis=0)
    inv = lax.rsqrt((got[:, 512] + got[:, 513] + got[:, 514]) / D + EPSILON)
    logits = got[:, :512] * inv[:, None]
    top = jnp.max(logits, axis=1)
    e = jnp.exp(logits - top[:, None])
    columns = t * vocab_local + lax.iota(jnp.int32, vocab_local)
    matches = targets[:, None] == columns[None, :]
    stats = jnp.stack(
        [
            top,
            jnp.sum(e, axis=1),
            jnp.sum(e * logits, axis=1),
            jnp.sum(jnp.where(matches, logits, 0.0), axis=1),
        ]
    ).reshape(1, 128)
    stats = spread(stats, TENSOR, 32).reshape(32, 4, 32)
    tops = stats[:, 0]
    global_top = jnp.max(tops, axis=0)
    scale = jnp.exp(tops - global_top)
    total = jnp.sum(stats[:, 1] * scale, axis=0)
    mean = jnp.sum(stats[:, 2] * scale, axis=0) / total
    inner = token_weight * (mean - jnp.sum(stats[:, 3], axis=0)) / D
    here = jnp.exp(logits - global_top[:, None]) / total[:, None]
    dlogits = ((here - matches.astype(f32)) * token_weight[:, None]).astype(bf16)
    gate_float = gate_pre.astype(f32)
    up_float = up_pre.astype(f32)
    sigmoid_gate = jax.nn.sigmoid(gate_float)
    hidden = (gate_float * sigmoid_gate * up_float).astype(bf16)
    scalars = jnp.pad(
        jnp.concatenate([split3(inv), split3(inner)], axis=1), ((0, 0), (0, 58))
    )
    sent = jnp.concatenate([dlogits, hidden, scalars], axis=1)
    got = spread(sent, DP, 16).reshape(512, 1024)
    piece = got[:, :512]
    hidden_all = got[:, 512:960]
    inv_all = join3(got[:, 960:963])
    inner_all = join3(got[:, 963:966])
    normed_all = (x_all * inv_all[:, None] * norm_gain).astype(bf16)
    weight_part = jnp.einsum("tv,td->vd", piece, normed_all, preferred_element_type=f32)
    mixed = piece.reshape(FARS, NEARS, 16, vocab_local).transpose(1, 0, 2, 3)
    mixed = lax.optimization_barrier(mixed.reshape(512, vocab_local))
    back_rows = jnp.dot(mixed, head_weight, preferred_element_type=f32)
    normed_back = scatter_tensor(back_rows)
    inv_own = lax.dynamic_slice_in_dim(inv_all, t * 16, 16)[:, None]
    inner_own = lax.dynamic_slice_in_dim(inner_all, t * 16, 16)[:, None]
    unit_rows = stream.astype(f32) * inv_own
    stream_grad = (inv_own * (normed_back * norm_gain - unit_rows * inner_own)).astype(bf16)
    gain_part = jnp.sum(normed_back * unit_rows, axis=0)
    stream_all, gain_grad = gather_and_sum(stream_grad, gain_part)
    stream_all = lax.optimization_barrier(in_order(stream_all))
    hidden_part = jnp.einsum(
        "td,fd->tf", stream_all, down_weight, preferred_element_type=f32
    ).astype(bf16)
    hidden_back = jnp.sum(exchange(hidden_part.reshape(16, 32, 448), DP).astype(f32), axis=0)
    down_grad = jnp.einsum("tf,td->fd", hidden_all, stream_all, preferred_element_type=f32)
    up_grad = (hidden_back * gate_float * sigmoid_gate).astype(bf16)
    gate_grad = (
        hidden_back * up_float * sigmoid_gate * (1.0 + gate_float * (1.0 - sigmoid_gate))
    ).astype(bf16)
    return (weight_part, down_grad, stream_grad, gain_grad, gate_grad, up_grad)


def solution(mesh):
    fine = Mesh(mesh.devices.reshape(8, 2, 2, 2, 4, 2), ("zf", "zn", "yl", "yh", "x", "c"))
    return jax.shard_map(
        per_device,
        mesh=fine,
        in_specs=(
            P(TENSOR, DP),
            P(DP),
            P(TENSOR, DP),
            P(TENSOR, DP),
            P(DP, TENSOR),
            P(DP, TENSOR),
            P(DP),
            P(DP),
        ),
        out_specs=(
            P(TENSOR, DP),
            P(TENSOR, DP),
            P(TENSOR, DP),
            P(DP),
            P(DP, TENSOR),
            P(DP, TENSOR),
        ),
        check_vma=False,
    )
```

```python
import jax
import jax.numpy as jnp
from jax import lax
from jax.experimental import pallas as pl
from jax.experimental.pallas import tpu as pltpu
from jax.sharding import Mesh, PartitionSpec as P

D = 12288
EPSILON = 1e-05
FAR, NEAR = ("zf",), ("zn", "yl")
TENSOR = FAR + NEAR
DP = ("yh", "x", "c")
FARS, NEARS = 8, 4
f32, bf16 = jnp.float32, jnp.bfloat16


def on_core(kernel, outs, *args, flops=0):
    whole = pl.BlockSpec(memory_space=pltpu.VMEM)
    outs = [jax.ShapeDtypeStruct(s, d) for s, d in outs]
    moved = sum(a.size * a.dtype.itemsize for a in list(args) + outs)
    return pl.pallas_call(
        kernel,
        out_shape=outs,
        in_specs=[whole] * len(args),
        out_specs=[whole] * len(outs),
        compiler_params=pltpu.CompilerParams(vmem_limit_bytes=16 << 20),
        cost_estimate=pl.CostEstimate(flops=flops, bytes_accessed=moved, transcendentals=0),
    )(*args)


def exchange(blocks, axes):
    return lax.all_to_all(blocks, axes, 0, 0, tiled=True)


def spread(block, axes, n):
    return exchange(jnp.broadcast_to(block[None], (n,) + block.shape), axes)


def gather_tensor(block):
    return spread(spread(block, FAR, FARS), NEAR, NEARS)


def in_order(blocks):
    return blocks.transpose(1, 0, 2, 3).reshape(-1, blocks.shape[-1])


def scatter_tensor(partial):
    rows, columns = partial.shape[0] // 32, partial.shape[1]
    near = exchange(partial.reshape(NEARS, FARS, rows, columns).astype(bf16), NEAR)
    near = jnp.sum(near.astype(f32), axis=0).astype(bf16)
    far = exchange(near, FAR)
    return jnp.sum(far.astype(f32), axis=0)


def split3(v):
    hi = lax.reduce_precision(v, 8, 7)
    mid = lax.reduce_precision(v - hi, 8, 7)
    lo = lax.reduce_precision(v - hi - mid, 8, 7)
    return jnp.stack([hi, mid, lo], axis=-1).astype(bf16)


def join3(s):
    s = s.astype(f32)
    return s[..., 0] + s[..., 1] + s[..., 2]


def gather_and_sum(block, term):
    n, columns = block.shape
    pair = split3(term)[:, :2].T.reshape(2 * columns // 128, 128)
    side = jnp.pad(pair, ((0, n - pair.shape[0]), (0, 0)))
    far = spread(jnp.concatenate([block, side], axis=1), FAR, FARS)
    side = far[:, : pair.shape[0], columns:].astype(f32).reshape(FARS, 2, columns)
    term = jnp.sum(side, axis=(0, 1))
    rows = far[:, :, :columns].reshape(FARS * n, columns)
    extra = jnp.pad(split3(term).T, ((0, 5), (0, 0)))
    return spread(jnp.concatenate([rows, extra], axis=0), NEAR, NEARS)


def token_rows(ref, first, count):
    return jnp.concatenate(
        [ref[n, f * 16 : f * 16 + 16] for f in range(first, first + count) for n in range(NEARS)]
    )


def columns_of(parts, width):
    lane = lax.broadcasted_iota(jnp.int32, (parts[0].shape[0], width), 1)
    out = jnp.zeros((parts[0].shape[0], width), f32)
    for k, part in enumerate(parts):
        out = jnp.where(lane == k, part, out)
    return out


def thirds(v):
    hi = v.astype(bf16).astype(f32)
    mid = (v - hi).astype(bf16).astype(f32)
    return [hi, mid, v - hi - mid]


def logits_kernel(x_ref, gain_ref, weight_ref, out_ref):
    for half in range(2):
        x = token_rows(x_ref, 4 * half, 4).astype(f32)
        scaled = (x * gain_ref[...]).astype(bf16)
        part = lax.dot_general(
            scaled, weight_ref[...], (((1,), (1,)), ((), ())), preferred_element_type=f32
        )
        rows = pl.ds(256 * half, 256)
        out_ref[rows, :512] = part.astype(bf16)
        squares = jnp.sum(x * x, axis=1, keepdims=True)
        out_ref[rows, 512:] = columns_of(thirds(squares), 128).astype(bf16)


def row_of(columns):
    lane = lax.broadcasted_iota(jnp.int32, (32, 128), 1)
    token = lax.broadcasted_iota(jnp.int32, (32, 128), 0)
    spreaded = jnp.zeros((32, 128), f32)
    for k, column in enumerate(columns):
        spreaded = jnp.where(lane == token + 32 * k, column, spreaded)
    return jnp.sum(spreaded, axis=0, keepdims=True)


def column_of(row):
    lane = lax.broadcasted_iota(jnp.int32, (32, 128), 1)
    token = lax.broadcasted_iota(jnp.int32, (32, 128), 0)
    return jnp.sum(jnp.where(lane == token, row, 0.0), axis=1, keepdims=True)


def stats_kernel(got_ref, mark_ref, logits_ref, inv_ref, stats_ref):
    total = jnp.zeros((32, 640), f32)
    for k in range(16):
        total = total + got_ref[k].astype(f32)
    squares = jnp.sum(total[:, 512:], axis=1, keepdims=True)
    inv = lax.rsqrt(squares / D + EPSILON)
    logits = total[:, :512] * inv
    top = jnp.max(logits, axis=1, keepdims=True)
    e = jnp.exp(logits - top)
    row = row_of(
        [
            top,
            jnp.sum(e, axis=1, keepdims=True),
            jnp.sum(e * logits, axis=1, keepdims=True),
            jnp.sum(logits * mark_ref[...], axis=1, keepdims=True),
        ]
    )
    logits_ref[...] = logits
    inv_ref[...] = jnp.broadcast_to(inv, (32, 128))
    stats_ref[...] = jnp.broadcast_to(row[None], (32, 1, 128))


def dlogits_kernel(stats_ref, logits_ref, inv_ref, mark_ref, weight_ref, hidden_ref, out_ref):
    stats = stats_ref[...].reshape(32, 128)
    lane = lax.broadcasted_iota(jnp.int32, (32, 128), 1)
    top = jnp.max(stats, axis=0, keepdims=True)
    scale = jnp.exp(jnp.where(lane < 32, stats - top, 0.0))
    sums = pltpu.roll(stats, 96, 1)
    means = pltpu.roll(stats, 64, 1)
    picked = pltpu.roll(stats, 32, 1)
    total = jnp.sum(sums * scale, axis=0, keepdims=True)
    mean = jnp.sum(means * scale, axis=0, keepdims=True) / total
    inner = mean - jnp.sum(picked, axis=0, keepdims=True)
    weight = weight_ref[:, :1]
    top, total, inner = column_of(top), column_of(total), column_of(inner) * weight / D
    probability = jnp.exp(logits_ref[...] - top) / total
    dlogits = ((probability - mark_ref[...]) * weight).astype(bf16)
    tail = columns_of(thirds(inv_ref[:, :1]) + thirds(inner), 64).astype(bf16)
    for k in range(16):
        out_ref[k, :, :512] = dlogits
        out_ref[k, :, 512:960] = hidden_ref[...]
        out_ref[k, :, 960:] = tail


def hidden_back_kernel(rows_ref, weight_ref, out_ref):
    for half in range(2):
        part = lax.dot_general(
            token_rows(rows_ref, 4 * half, 4),
            weight_ref[...],
            (((1,), (1,)), ((), ())),
            preferred_element_type=f32,
        )
        out_ref[pl.ds(256 * half, 256), :] = part.astype(bf16)


def per_device(
    stream, norm_gain, head_weight, down_weight, gate_pre, up_pre, targets, token_weight
):
    vocab_local = head_weight.shape[0]
    t = lax.axis_index(TENSOR)
    gate_float = gate_pre.astype(f32)
    up_float = up_pre.astype(f32)
    sigmoid_gate = jax.nn.sigmoid(gate_float)
    hidden = (gate_float * sigmoid_gate * up_float).astype(bf16)
    columns = t * vocab_local + lax.iota(jnp.int32, vocab_local)
    matches = (targets[:, None] == columns[None, :]).astype(f32)
    own = t.astype(jnp.uint32) * 16
    first, stream_float, gain_row, gain_rows, hidden, matches, weight, own = (
        lax.optimization_barrier(
            (
                stream,
                stream.astype(f32),
                norm_gain[None],
                jnp.broadcast_to(norm_gain, stream.shape),
                hidden,
                matches,
                jnp.broadcast_to(token_weight[:, None], (32, 128)),
                own,
            )
        )
    )
    x_blocks = gather_tensor(first)
    part = on_core(
        logits_kernel,
        [((512, 640), bf16)],
        x_blocks.reshape(NEARS, FARS * 16, 768),
        gain_row,
        head_weight,
        flops=2 * 512 * 512 * 768,
    )[0]
    got = exchange(part.reshape(16, 32, 640), DP)
    logits, inv, stats = on_core(
        stats_kernel,
        [((32, 512), f32), ((32, 128), f32), ((32, 1, 128), f32)],
        got,
        matches,
    )
    stats = exchange(stats, TENSOR)
    sent = on_core(
        dlogits_kernel, [((16, 32, 1024), bf16)], stats, logits, inv, matches, weight, hidden
    )[0]
    got = exchange(sent, DP).reshape(512, 1024)
    piece = got[:, :512]
    inv_all = join3(got[:, 960:963])
    inner_all = join3(got[:, 963:966])
    inv_own = lax.dynamic_slice_in_dim(inv_all, own, 16)[:, None]
    inner_own = lax.dynamic_slice_in_dim(inner_all, own, 16)[:, None]
    mixed = piece.reshape(FARS, NEARS, 16, vocab_local).transpose(1, 0, 2, 3)
    unit_rows = stream_float * inv_own
    grown, pulled = inv_own * gain_rows, inv_own * inner_own * unit_rows
    mixed, unit_rows, grown, pulled = lax.optimization_barrier(
        (mixed.reshape(512, vocab_local), unit_rows, grown, pulled)
    )
    back_rows = jnp.dot(mixed, head_weight, preferred_element_type=f32)
    normed_back = scatter_tensor(back_rows)
    stream_grad = (normed_back * grown - pulled).astype(bf16)
    gathered = gather_and_sum(stream_grad, jnp.sum(normed_back * unit_rows, axis=0))
    hidden_part = on_core(
        hidden_back_kernel,
        [((512, 448), bf16)],
        gathered,
        down_weight,
        flops=2 * 512 * 448 * 768,
    )[0]
    gathered, inv_all, x_blocks = lax.optimization_barrier((gathered, inv_all, x_blocks))
    gain_grad = jnp.sum(gathered[:, 128:131].astype(f32), axis=(0, 1))
    stream_all = in_order(gathered[:, :128].reshape(NEARS, FARS, 16, 768))
    x_all = in_order(x_blocks).astype(f32)
    normed_all = (x_all * inv_all[:, None] * norm_gain).astype(bf16)
    weight_part = jnp.einsum("tv,td->vd", piece, normed_all, preferred_element_type=f32)
    down_grad = jnp.einsum("tf,td->fd", got[:, 512:960], stream_all, preferred_element_type=f32)
    hidden_back = jnp.sum(exchange(hidden_part.reshape(16, 32, 448), DP).astype(f32), axis=0)
    up_grad = (hidden_back * gate_float * sigmoid_gate).astype(bf16)
    gate_grad = (
        hidden_back * up_float * sigmoid_gate * (1.0 + gate_float * (1.0 - sigmoid_gate))
    ).astype(bf16)
    return (weight_part, down_grad, stream_grad, gain_grad, gate_grad, up_grad)


def solution(mesh):
    fine = Mesh(mesh.devices.reshape(8, 2, 2, 2, 4, 2), ("zf", "zn", "yl", "yh", "x", "c"))
    return jax.shard_map(
        per_device,
        mesh=fine,
        in_specs=(
            P(TENSOR, DP),
            P(DP),
            P(TENSOR, DP),
            P(TENSOR, DP),
            P(DP, TENSOR),
            P(DP, TENSOR),
            P(DP),
            P(DP),
        ),
        out_specs=(
            P(TENSOR, DP),
            P(TENSOR, DP),
            P(TENSOR, DP),
            P(DP),
            P(DP, TENSOR),
            P(DP, TENSOR),
        ),
        check_vma=False,
    )
```

```python
import jax
import jax.numpy as jnp
from jax import lax
from jax.experimental import pallas as pl
from jax.experimental.pallas import tpu as pltpu
from jax.sharding import Mesh, PartitionSpec as P

D = 12288
EPSILON = 1e-05
FAR, NEAR = ("zf",), ("zn", "yl")
TENSOR = FAR + NEAR
CHIPS = ("yh", "x")
DP = CHIPS + ("c",)
FARS, NEARS = 8, 4
f32, bf16 = jnp.float32, jnp.bfloat16


def on_core(kernel, outs, *args, flops=0):
    whole = pl.BlockSpec(memory_space=pltpu.VMEM)
    outs = [jax.ShapeDtypeStruct(s, d) for s, d in outs]
    moved = sum(a.size * a.dtype.itemsize for a in list(args) + outs)
    return pl.pallas_call(
        kernel,
        out_shape=outs,
        in_specs=[
            pl.BlockSpec(memory_space=pltpu.SMEM) if a.shape == (1,) else whole for a in args
        ],
        out_specs=[whole] * len(outs),
        compiler_params=pltpu.CompilerParams(vmem_limit_bytes=16 << 20),
        cost_estimate=pl.CostEstimate(flops=flops, bytes_accessed=moved, transcendentals=0),
    )(*args)


def exchange(blocks, axes):
    return lax.all_to_all(blocks, axes, 0, 0, tiled=True)


def spread(block, axes, n):
    return exchange(jnp.broadcast_to(block[None], (n,) + block.shape), axes)


def other_core(block):
    return lax.ppermute(block, "c", [(0, 1), (1, 0)])


def split3(v):
    hi = lax.reduce_precision(v, 8, 7)
    mid = lax.reduce_precision(v - hi, 8, 7)
    lo = lax.reduce_precision(v - hi - mid, 8, 7)
    return jnp.stack([hi, mid, lo], axis=-1).astype(bf16)


def near_gather(far):
    side = far[:, :12, 768:].astype(f32).reshape(FARS, 2, 768)
    rows = far[:, :, :768].reshape(FARS * 16, 768)
    extra = jnp.pad(split3(jnp.sum(side, axis=(0, 1))).T, ((0, 5), (0, 0)))
    return spread(jnp.concatenate([rows, extra], axis=0), NEAR, NEARS)


def token_rows(ref, first, count):
    return jnp.concatenate(
        [ref[n, f * 16 : f * 16 + 16] for f in range(first, first + count) for n in range(NEARS)]
    )


def columns_of(parts, width):
    lane = lax.broadcasted_iota(jnp.int32, (parts[0].shape[0], width), 1)
    out = jnp.zeros((parts[0].shape[0], width), f32)
    for k, part in enumerate(parts):
        out = jnp.where(lane == k, part, out)
    return out


def thirds(v):
    hi = v.astype(bf16).astype(f32)
    mid = (v - hi).astype(bf16).astype(f32)
    return [hi, mid, v - hi - mid]


def logits_kernel(x_ref, gain_ref, weight_ref, out_ref):
    gain = gain_ref[...].reshape(1, 768)
    for half in range(2):
        x = token_rows(x_ref, 4 * half, 4).astype(f32)
        scaled = (x * gain).astype(bf16)
        part = lax.dot_general(
            scaled, weight_ref[...], (((1,), (1,)), ((), ())), preferred_element_type=f32
        )
        rows = pl.ds(256 * half, 256)
        out_ref[rows, :512] = part.astype(bf16)
        squares = jnp.sum(x * x, axis=1, keepdims=True)
        out_ref[rows, 512:] = columns_of(thirds(squares), 128).astype(bf16)


def row_of(columns):
    lane = lax.broadcasted_iota(jnp.int32, (32, 128), 1)
    token = lax.broadcasted_iota(jnp.int32, (32, 128), 0)
    spreaded = jnp.zeros((32, 128), f32)
    for k, column in enumerate(columns):
        spreaded = jnp.where(lane == token + 32 * k, column, spreaded)
    return jnp.sum(spreaded, axis=0, keepdims=True)


def column_of(row):
    lane = lax.broadcasted_iota(jnp.int32, (32, 128), 1)
    token = lax.broadcasted_iota(jnp.int32, (32, 128), 0)
    return jnp.sum(jnp.where(lane == token, row, 0.0), axis=1, keepdims=True)


def column(ref):
    row = ref[...].astype(f32).reshape(1, 32)
    lane = lax.broadcasted_iota(jnp.int32, (32, 32), 1)
    token = lax.broadcasted_iota(jnp.int32, (32, 32), 0)
    return jnp.sum(jnp.where(lane == token, row, 0.0), axis=1, keepdims=True)


def stats_kernel(
    first_ref, got_ref, targets_ref, weight_ref, logits_ref, scale_ref, stats_ref, mark_ref
):
    at = column(targets_ref).astype(jnp.int32) - first_ref[0]
    mark = (lax.broadcasted_iota(jnp.int32, (32, 512), 1) == at).astype(f32)
    total = jnp.zeros((32, 640), f32)
    for k in range(16):
        total = total + got_ref[k].astype(f32)
    squares = jnp.sum(total[:, 512:], axis=1, keepdims=True)
    inv = lax.rsqrt(squares / D + EPSILON)
    logits = total[:, :512] * inv
    top = jnp.max(logits, axis=1, keepdims=True)
    e = jnp.exp(logits - top)
    row = row_of(
        [
            top,
            jnp.sum(e, axis=1, keepdims=True),
            jnp.sum(e * logits, axis=1, keepdims=True),
            jnp.sum(logits * mark, axis=1, keepdims=True),
        ]
    )
    logits_ref[...] = logits
    scale_ref[...] = columns_of([inv, column(weight_ref)], 128)
    mark_ref[...] = mark
    stats_ref[...] = jnp.broadcast_to(row[None], (32, 1, 128))


def dlogits_kernel(stats_ref, logits_ref, scale_ref, mark_ref, gate_ref, up_ref, out_ref):
    gate, up = gate_ref[...].astype(f32), up_ref[...].astype(f32)
    hidden = (gate * jax.nn.sigmoid(gate) * up).astype(bf16)
    stats = stats_ref[...].reshape(32, 128)
    lane = lax.broadcasted_iota(jnp.int32, (32, 128), 1)
    top = jnp.max(stats, axis=0, keepdims=True)
    scale = jnp.exp(jnp.where(lane < 32, stats - top, 0.0))
    sums = pltpu.roll(stats, 96, 1)
    means = pltpu.roll(stats, 64, 1)
    picked = pltpu.roll(stats, 32, 1)
    total = jnp.sum(sums * scale, axis=0, keepdims=True)
    mean = jnp.sum(means * scale, axis=0, keepdims=True) / total
    inner = mean - jnp.sum(picked, axis=0, keepdims=True)
    weight = scale_ref[:, 1:2]
    top, total, inner = column_of(top), column_of(total), column_of(inner) * weight / D
    probability = jnp.exp(logits_ref[...] - top) / total
    dlogits = ((probability - mark_ref[...]) * weight).astype(bf16)
    tail = columns_of(thirds(scale_ref[:, :1]) + thirds(inner), 64).astype(bf16)
    for k in range(8):
        out_ref[k, :, :512] = dlogits
        out_ref[k, :, 512:960] = hidden
        out_ref[k, :, 960:] = tail


def half_rows(core_ref, side, mine_ref, others_ref, lanes):
    here = core_ref[0] == side
    return jnp.concatenate(
        [
            jnp.where(here, mine_ref[f, y : y + 16, lanes], others_ref[f, y : y + 16, lanes])
            for y in (0, 16)
            for f in range(FARS)
        ]
    )


def back_kernel(core_ref, mine_ref, others_ref, weight_ref, out_ref):
    for side in range(2):
        rows = half_rows(core_ref, side, mine_ref, others_ref, slice(0, 512))
        part = jnp.dot(rows, weight_ref[...], preferred_element_type=f32)
        out_ref[2 * side] = part[:128].astype(bf16)
        out_ref[2 * side + 1] = part[128:].astype(bf16)


def weights_kernel(
    core_ref, mine_ref, others_ref, x_ref, gain_ref, rows_ref, head_ref, down_ref
):
    def add(ref, side, a, b):
        part = lax.dot_general(a, b, (((0,), (0,)), ((), ())), preferred_element_type=f32)
        ref[...] = part if side == 0 else ref[...] + part

    for side in range(2):
        got = half_rows(core_ref, side, mine_ref, others_ref, slice(0, 1024))
        tail = got[:, 896:].astype(f32)
        inv = tail[:, 64:65] + tail[:, 65:66] + tail[:, 66:67]
        x = x_ref[2 * side : 2 * side + 2].reshape(256, 768).astype(f32)
        normed = (x * inv * gain_ref[...].reshape(1, 768)).astype(bf16)
        add(head_ref, side, got[:, :512], normed)
        rows = rows_ref[2 * side : 2 * side + 2, :128].reshape(256, 768)
        add(down_ref, side, got[:, 512:960], rows)


def grad_kernel(
    core_ref, near_ref, far_ref, low_ref, got_ref, mine_ref, others_ref, x_ref, gain_ref,
    out_ref,
):
    rows = pl.ds(pl.multiple_of(low_ref[0] * 16, 16), 16)
    here = core_ref[0] == near_ref[0]
    tail = jnp.where(
        here, mine_ref[far_ref[0], rows, 896:], others_ref[far_ref[0], rows, 896:]
    ).astype(f32)
    inv = tail[:, 64:65] + tail[:, 65:66] + tail[:, 66:67]
    inner = tail[:, 67:68] + tail[:, 68:69] + tail[:, 69:70]
    normed_back = jnp.zeros((16, 768), f32)
    for k in range(FARS):
        normed_back = normed_back + got_ref[k].astype(f32)
    unit_rows = x_ref[...].astype(f32) * inv
    grad = (inv * (normed_back * gain_ref[...].reshape(1, 768) - unit_rows * inner)).astype(bf16)
    term = thirds(jnp.sum(normed_back * unit_rows, axis=0, keepdims=True))
    row = lax.broadcasted_iota(jnp.int32, (16, 128), 0)
    side = jnp.zeros((16, 128), f32)
    for k in range(12):
        piece = term[k // 6][:, k % 6 * 128 : k % 6 * 128 + 128]
        side = jnp.where(row == k, piece, side)
    for k in range(FARS):
        out_ref[k, :, :768] = grad
        out_ref[k, :, 768:] = side.astype(bf16)


def hidden_back_kernel(rows_ref, weight_ref, out_ref):
    for half in range(2):
        part = lax.dot_general(
            token_rows(rows_ref, 4 * half, 4),
            weight_ref[...],
            (((1,), (1,)), ((), ())),
            preferred_element_type=f32,
        )
        out_ref[pl.ds(256 * half, 256), :] = part.astype(bf16)


def per_device(
    stream, norm_gain, head_weight, down_weight, gate_pre, up_pre, targets, token_weight
):
    vocab_local = head_weight.shape[0]
    t = lax.axis_index(TENSOR)
    first = (t * vocab_local).astype(jnp.int32)[None]
    places = [lax.axis_index(a).astype(jnp.int32)[None] for a in ("c", "zn", "zf", "yl")]
    rows, first, places = lax.optimization_barrier((stream, first, places))
    core = places[0]
    far = spread(rows, FAR, FARS)
    x_blocks = spread(far, NEAR, NEARS)
    part = on_core(
        logits_kernel,
        [((512, 640), bf16)],
        x_blocks.reshape(NEARS, FARS * 16, 768),
        norm_gain,
        head_weight,
        flops=2 * 512 * 512 * 768,
    )[0]
    got = exchange(part.reshape(16, 32, 640), DP)
    logits, scale, stats, mark = on_core(
        stats_kernel,
        [((32, 512), f32), ((32, 128), f32), ((32, 1, 128), f32), ((32, 512), f32)],
        first,
        got,
        targets,
        token_weight,
    )
    stats = exchange(stats, TENSOR)
    sent = on_core(
        dlogits_kernel, [((8, 32, 1024), bf16)], stats, logits, scale, mark, gate_pre, up_pre
    )[0]
    mine = exchange(sent, CHIPS)
    others = other_core(mine)

    back = on_core(
        back_kernel,
        [((NEARS, FARS * 16, 768), bf16)],
        core,
        mine,
        others,
        head_weight,
        flops=2 * 512 * 512 * 768,
    )[0]
    near = jnp.sum(exchange(back, NEAR).astype(f32), axis=0).astype(bf16)
    got = exchange(near.reshape(FARS, 16, 768), FAR)
    sent = on_core(
        grad_kernel,
        [((FARS, 16, 896), bf16)],
        *places,
        got,
        mine,
        others,
        stream,
        norm_gain,
    )[0]
    gathered = near_gather(exchange(sent, FAR))
    hidden_part = on_core(
        hidden_back_kernel,
        [((512, 448), bf16)],
        gathered,
        down_weight,
        flops=2 * 512 * 448 * 768,
    )[0]
    gathered, sent, x_blocks, mine, others, hidden_part = lax.optimization_barrier(
        (gathered, sent, x_blocks, mine, others, hidden_part)
    )
    stream_grad = sent[0, :, :768]
    gain_grad = jnp.sum(gathered[:, 128:131].astype(f32), axis=(0, 1))
    head_grad, down_grad = on_core(
        weights_kernel,
        [((512, 768), f32), ((448, 768), f32)],
        core,
        mine,
        others,
        x_blocks.reshape(NEARS, FARS * 16, 768),
        norm_gain,
        gathered,
        flops=2 * 512 * 960 * 768,
    )
    hidden_back = jnp.sum(exchange(hidden_part.reshape(16, 32, 448), DP).astype(f32), axis=0)
    gate_float = gate_pre.astype(f32)
    up_float = up_pre.astype(f32)
    sigmoid_gate = jax.nn.sigmoid(gate_float)
    up_grad = (hidden_back * gate_float * sigmoid_gate).astype(bf16)
    gate_grad = (
        hidden_back * up_float * sigmoid_gate * (1.0 + gate_float * (1.0 - sigmoid_gate))
    ).astype(bf16)
    return (head_grad, down_grad, stream_grad, gain_grad, gate_grad, up_grad)


def solution(mesh):
    fine = Mesh(mesh.devices.reshape(8, 2, 2, 2, 4, 2), ("zf", "zn", "yl", "yh", "x", "c"))
    return jax.shard_map(
        per_device,
        mesh=fine,
        in_specs=(
            P(TENSOR, DP),
            P(DP),
            P(TENSOR, DP),
            P(TENSOR, DP),
            P(DP, TENSOR),
            P(DP, TENSOR),
            P(DP),
            P(DP),
        ),
        out_specs=(
            P(TENSOR, DP),
            P(TENSOR, DP),
            P(TENSOR, DP),
            P(DP),
            P(DP, TENSOR),
            P(DP, TENSOR),
        ),
        check_vma=False,
    )
```

```python
import jax
import jax.numpy as jnp
from jax import lax
from jax.experimental import pallas as pl
from jax.experimental.pallas import tpu as pltpu
from jax.sharding import Mesh, PartitionSpec as P

D = 12288
EPSILON = 1e-05
FAR, NEAR = ("zf",), ("zn", "yl")
TENSOR = FAR + NEAR
CHIPS = ("yh", "x")
DP = CHIPS + ("c",)
FARS, NEARS = 8, 4
f32, bf16 = jnp.float32, jnp.bfloat16


def on_core(kernel, outs, *args, flops=0):
    whole = pl.BlockSpec(memory_space=pltpu.VMEM)
    outs = [jax.ShapeDtypeStruct(s, d) for s, d in outs]
    moved = sum(a.size * a.dtype.itemsize for a in list(args) + outs)
    return pl.pallas_call(
        kernel,
        out_shape=outs,
        in_specs=[
            pl.BlockSpec(memory_space=pltpu.SMEM) if a.shape == (1,) else whole for a in args
        ],
        out_specs=[whole] * len(outs),
        compiler_params=pltpu.CompilerParams(vmem_limit_bytes=16 << 20),
        cost_estimate=pl.CostEstimate(flops=flops, bytes_accessed=moved, transcendentals=0),
    )(*args)


def exchange(blocks, axes):
    return lax.all_to_all(blocks, axes, 0, 0, tiled=True)


def spread(block, axes, n):
    return exchange(jnp.broadcast_to(block[None], (n,) + block.shape), axes)


def other_core(block):
    return lax.ppermute(block, "c", [(0, 1), (1, 0)])


def token_rows(ref, first, count):
    return jnp.concatenate(
        [ref[n, f * 16 : f * 16 + 16] for f in range(first, first + count) for n in range(NEARS)]
    )


def columns_of(parts, width):
    lane = lax.broadcasted_iota(jnp.int32, (parts[0].shape[0], width), 1)
    out = jnp.zeros((parts[0].shape[0], width), f32)
    for k, part in enumerate(parts):
        out = jnp.where(lane == k, part, out)
    return out


def thirds(v):
    hi = v.astype(bf16).astype(f32)
    mid = (v - hi).astype(bf16).astype(f32)
    return [hi, mid, v - hi - mid]


def logits_kernel(x_ref, gain_ref, weight_ref, out_ref):
    gain = gain_ref[...].reshape(1, 768)
    for half in range(2):
        x = token_rows(x_ref, 4 * half, 4).astype(f32)
        scaled = (x * gain).astype(bf16)
        part = lax.dot_general(
            scaled, weight_ref[...], (((1,), (1,)), ((), ())), preferred_element_type=f32
        )
        rows = pl.ds(256 * half, 256)
        out_ref[rows, :512] = part.astype(bf16)
        squares = jnp.sum(x * x, axis=1, keepdims=True)
        out_ref[rows, 512:] = columns_of(thirds(squares), 128).astype(bf16)


def row_of(columns):
    lane = lax.broadcasted_iota(jnp.int32, (32, 128), 1)
    token = lax.broadcasted_iota(jnp.int32, (32, 128), 0)
    spreaded = jnp.zeros((32, 128), f32)
    for k, column in enumerate(columns):
        spreaded = jnp.where(lane == token + 32 * k, column, spreaded)
    return jnp.sum(spreaded, axis=0, keepdims=True)


def column_of(row):
    lane = lax.broadcasted_iota(jnp.int32, (32, 128), 1)
    token = lax.broadcasted_iota(jnp.int32, (32, 128), 0)
    return jnp.sum(jnp.where(lane == token, row, 0.0), axis=1, keepdims=True)


def column(ref):
    row = ref[...].astype(f32).reshape(1, 32)
    lane = lax.broadcasted_iota(jnp.int32, (32, 32), 1)
    token = lax.broadcasted_iota(jnp.int32, (32, 32), 0)
    return jnp.sum(jnp.where(lane == token, row, 0.0), axis=1, keepdims=True)


def stats_kernel(
    first_ref, got_ref, targets_ref, weight_ref, logits_ref, scale_ref, stats_ref, mark_ref
):
    at = column(targets_ref).astype(jnp.int32) - first_ref[0]
    mark = (lax.broadcasted_iota(jnp.int32, (32, 512), 1) == at).astype(f32)
    total = jnp.zeros((32, 640), f32)
    for k in range(16):
        total = total + got_ref[k].astype(f32)
    squares = jnp.sum(total[:, 512:], axis=1, keepdims=True)
    inv = lax.rsqrt(squares / D + EPSILON)
    logits = total[:, :512] * inv
    top = jnp.max(logits, axis=1, keepdims=True)
    e = jnp.exp(logits - top)
    row = row_of(
        [
            top,
            jnp.sum(e, axis=1, keepdims=True),
            jnp.sum(e * logits, axis=1, keepdims=True),
            jnp.sum(logits * mark, axis=1, keepdims=True),
        ]
    )
    logits_ref[...] = logits
    scale_ref[...] = columns_of([inv, column(weight_ref)], 128)
    mark_ref[...] = mark
    stats_ref[...] = jnp.broadcast_to(row[None], (32, 1, 128))


def dlogits_kernel(stats_ref, logits_ref, scale_ref, mark_ref, gate_ref, up_ref, out_ref):
    gate, up = gate_ref[...].astype(f32), up_ref[...].astype(f32)
    hidden = (gate * jax.nn.sigmoid(gate) * up).astype(bf16)
    stats = stats_ref[...].reshape(32, 128)
    lane = lax.broadcasted_iota(jnp.int32, (32, 128), 1)
    top = jnp.max(stats, axis=0, keepdims=True)
    scale = jnp.exp(jnp.where(lane < 32, stats - top, 0.0))
    sums = pltpu.roll(stats, 96, 1)
    means = pltpu.roll(stats, 64, 1)
    picked = pltpu.roll(stats, 32, 1)
    total = jnp.sum(sums * scale, axis=0, keepdims=True)
    mean = jnp.sum(means * scale, axis=0, keepdims=True) / total
    inner = mean - jnp.sum(picked, axis=0, keepdims=True)
    weight = scale_ref[:, 1:2]
    top, total, inner = column_of(top), column_of(total), column_of(inner) * weight / D
    probability = jnp.exp(logits_ref[...] - top) / total
    dlogits = ((probability - mark_ref[...]) * weight).astype(bf16)
    tail = columns_of(thirds(scale_ref[:, :1]) + thirds(inner), 64).astype(bf16)
    for k in range(8):
        out_ref[k, :, :512] = dlogits
        out_ref[k, :, 512:960] = hidden
        out_ref[k, :, 960:] = tail


def half_rows(core_ref, side, mine_ref, others_ref, lanes):
    here = core_ref[0] == side
    return jnp.concatenate(
        [
            jnp.where(here, mine_ref[f, y : y + 16, lanes], others_ref[f, y : y + 16, lanes])
            for y in (0, 16)
            for f in range(FARS)
        ]
    )


def back_kernel(core_ref, mine_ref, others_ref, weight_ref, out_ref):
    for side in range(2):
        rows = half_rows(core_ref, side, mine_ref, others_ref, slice(0, 512))
        part = jnp.dot(rows, weight_ref[...], preferred_element_type=f32)
        out_ref[2 * side] = part[:128].astype(bf16)
        out_ref[2 * side + 1] = part[128:].astype(bf16)


def weights_kernel(
    core_ref, mine_ref, others_ref, x_ref, gain_ref, rows_ref, head_ref, down_ref, sum_ref
):
    def add(ref, side, part):
        ref[...] = part if side == 0 else ref[...] + part

    def product(a, b):
        return lax.dot_general(a, b, (((0,), (0,)), ((), ())), preferred_element_type=f32)

    gain = gain_ref[...].reshape(1, 768)
    for side in range(2):
        got = half_rows(core_ref, side, mine_ref, others_ref, slice(0, 1024))
        tail = got[:, 896:].astype(f32)
        inv = tail[:, 64:65] + tail[:, 65:66] + tail[:, 66:67]
        inner = tail[:, 67:68] + tail[:, 68:69] + tail[:, 69:70]
        unit_rows = x_ref[2 * side : 2 * side + 2].reshape(256, 768).astype(f32) * inv
        add(head_ref, side, product(got[:, :512], (unit_rows * gain).astype(bf16)))
        rows = rows_ref[2 * side : 2 * side + 2].reshape(256, 768)
        add(down_ref, side, product(got[:, 512:960], rows))
        scaled = rows.astype(f32) * (1.0 / inv) + unit_rows * inner
        add(sum_ref, side, jnp.sum(scaled * unit_rows, axis=0, keepdims=True))
    sum_ref[...] = sum_ref[...] / gain


def grad_kernel(
    core_ref, near_ref, far_ref, low_ref, got_ref, mine_ref, others_ref, x_ref, gain_ref,
    out_ref,
):
    rows = pl.ds(pl.multiple_of(low_ref[0] * 16, 16), 16)
    here = core_ref[0] == near_ref[0]
    tail = jnp.where(
        here, mine_ref[far_ref[0], rows, 896:], others_ref[far_ref[0], rows, 896:]
    ).astype(f32)
    inv = tail[:, 64:65] + tail[:, 65:66] + tail[:, 66:67]
    inner = tail[:, 67:68] + tail[:, 68:69] + tail[:, 69:70]
    normed_back = jnp.zeros((16, 768), f32)
    for k in range(FARS):
        normed_back = normed_back + got_ref[k].astype(f32)
    unit_rows = x_ref[...].astype(f32) * inv
    grad = (inv * (normed_back * gain_ref[...].reshape(1, 768) - unit_rows * inner)).astype(bf16)
    for k in range(FARS):
        out_ref[k] = grad


def hidden_back_kernel(rows_ref, weight_ref, out_ref):
    for half in range(2):
        part = lax.dot_general(
            token_rows(rows_ref, 4 * half, 4),
            weight_ref[...],
            (((1,), (1,)), ((), ())),
            preferred_element_type=f32,
        )
        out_ref[pl.ds(256 * half, 256), :] = part.astype(bf16)


def per_device(
    stream, norm_gain, head_weight, down_weight, gate_pre, up_pre, targets, token_weight
):
    vocab_local = head_weight.shape[0]
    t = lax.axis_index(TENSOR)
    first = (t * vocab_local).astype(jnp.int32)[None]
    places = [lax.axis_index(a).astype(jnp.int32)[None] for a in ("c", "zn", "zf", "yl")]
    rows, first, places = lax.optimization_barrier((stream, first, places))
    core = places[0]
    far = spread(rows, FAR, FARS)
    x_blocks = spread(far, NEAR, NEARS)
    part = on_core(
        logits_kernel,
        [((512, 640), bf16)],
        x_blocks.reshape(NEARS, FARS * 16, 768),
        norm_gain,
        head_weight,
        flops=2 * 512 * 512 * 768,
    )[0]
    got = exchange(part.reshape(16, 32, 640), DP)
    logits, scale, stats, mark = on_core(
        stats_kernel,
        [((32, 512), f32), ((32, 128), f32), ((32, 1, 128), f32), ((32, 512), f32)],
        first,
        got,
        targets,
        token_weight,
    )
    stats = exchange(stats, TENSOR)
    sent = on_core(
        dlogits_kernel, [((8, 32, 1024), bf16)], stats, logits, scale, mark, gate_pre, up_pre
    )[0]
    mine = exchange(sent, CHIPS)
    others = other_core(mine)

    back = on_core(
        back_kernel,
        [((NEARS, FARS * 16, 768), bf16)],
        core,
        mine,
        others,
        head_weight,
        flops=2 * 512 * 512 * 768,
    )[0]
    near = jnp.sum(exchange(back, NEAR).astype(f32), axis=0).astype(bf16)
    got = exchange(near.reshape(FARS, 16, 768), FAR)
    sent = on_core(
        grad_kernel,
        [((FARS, 16, 768), bf16)],
        *places,
        got,
        mine,
        others,
        stream,
        norm_gain,
    )[0]
    gathered = spread(exchange(sent, FAR).reshape(FARS * 16, 768), NEAR, NEARS)
    hidden_part = on_core(
        hidden_back_kernel,
        [((512, 448), bf16)],
        gathered,
        down_weight,
        flops=2 * 512 * 448 * 768,
    )[0]
    gathered, sent, x_blocks, mine, others, hidden_part = lax.optimization_barrier(
        (gathered, sent, x_blocks, mine, others, hidden_part)
    )
    stream_grad = sent[0]
    head_grad, down_grad, gain_grad = on_core(
        weights_kernel,
        [((512, 768), f32), ((448, 768), f32), ((1, 768), f32)],
        core,
        mine,
        others,
        x_blocks.reshape(NEARS, FARS * 16, 768),
        norm_gain,
        gathered,
        flops=2 * 512 * 960 * 768,
    )
    hidden_back = jnp.sum(exchange(hidden_part.reshape(16, 32, 448), DP).astype(f32), axis=0)
    gate_float = gate_pre.astype(f32)
    up_float = up_pre.astype(f32)
    sigmoid_gate = jax.nn.sigmoid(gate_float)
    up_grad = (hidden_back * gate_float * sigmoid_gate).astype(bf16)
    gate_grad = (
        hidden_back * up_float * sigmoid_gate * (1.0 + gate_float * (1.0 - sigmoid_gate))
    ).astype(bf16)
    return (head_grad, down_grad, stream_grad, gain_grad[0], gate_grad, up_grad)


def solution(mesh):
    fine = Mesh(mesh.devices.reshape(8, 2, 2, 2, 4, 2), ("zf", "zn", "yl", "yh", "x", "c"))
    return jax.shard_map(
        per_device,
        mesh=fine,
        in_specs=(
            P(TENSOR, DP),
            P(DP),
            P(TENSOR, DP),
            P(TENSOR, DP),
            P(DP, TENSOR),
            P(DP, TENSOR),
            P(DP),
            P(DP),
        ),
        out_specs=(
            P(TENSOR, DP),
            P(TENSOR, DP),
            P(TENSOR, DP),
            P(DP),
            P(DP, TENSOR),
            P(DP, TENSOR),
        ),
        check_vma=False,
    )
```

```python
import jax
import jax.numpy as jnp
from jax import lax
from jax.experimental import pallas as pl
from jax.experimental.pallas import tpu as pltpu
from jax.sharding import Mesh, PartitionSpec as P

D = 12288
EPSILON = 1e-05
FAR, NEAR = ("zf",), ("zn", "yl")
TENSOR = FAR + NEAR
CHIPS = ("yh", "x")
DP = CHIPS + ("c",)
FARS, NEARS = 8, 4
f32, bf16 = jnp.float32, jnp.bfloat16


def on_core(kernel, outs, *args, flops=0):
    whole = pl.BlockSpec(memory_space=pltpu.VMEM)
    outs = [jax.ShapeDtypeStruct(s, d) for s, d in outs]
    moved = sum(a.size * a.dtype.itemsize for a in list(args) + outs)
    return pl.pallas_call(
        kernel,
        out_shape=outs,
        in_specs=[
            pl.BlockSpec(memory_space=pltpu.SMEM) if a.shape == (1,) else whole for a in args
        ],
        out_specs=[whole] * len(outs),
        compiler_params=pltpu.CompilerParams(vmem_limit_bytes=16 << 20),
        cost_estimate=pl.CostEstimate(flops=flops, bytes_accessed=moved, transcendentals=0),
    )(*args)


def exchange(blocks, axes):
    return lax.all_to_all(blocks, axes, 0, 0, tiled=True)


def spread(block, axes, n):
    return exchange(jnp.broadcast_to(block[None], (n,) + block.shape), axes)


def other_core(block):
    return lax.ppermute(block, "c", [(0, 1), (1, 0)])


def token_rows(ref, first, count):
    return jnp.concatenate(
        [ref[n, f * 16 : f * 16 + 16] for f in range(first, first + count) for n in range(NEARS)]
    )


def columns_of(parts, width):
    lane = lax.broadcasted_iota(jnp.int32, (parts[0].shape[0], width), 1)
    out = jnp.zeros((parts[0].shape[0], width), f32)
    for k, part in enumerate(parts):
        out = jnp.where(lane == k, part, out)
    return out


def thirds(v):
    hi = v.astype(bf16).astype(f32)
    mid = (v - hi).astype(bf16).astype(f32)
    return [hi, mid, v - hi - mid]


def logits_kernel(x_ref, gain_ref, weight_ref, out_ref):
    gain = gain_ref[...].reshape(1, 768)
    for half in range(2):
        x = token_rows(x_ref, 4 * half, 4).astype(f32)
        scaled = (x * gain).astype(bf16)
        part = lax.dot_general(
            scaled, weight_ref[...], (((1,), (1,)), ((), ())), preferred_element_type=f32
        )
        part = part.astype(bf16)
        squares = jnp.sum(x * x, axis=1, keepdims=True)
        for k in range(8):
            to, rows = 8 * half + k, slice(32 * k, 32 * k + 32)
            for j in range(4):
                out_ref[to, 32 * j : 32 * j + 32, :] = part[rows, 128 * j : 128 * j + 128]
            row = row_of(thirds(squares[rows]))
            out_ref[to, 128:, :] = jnp.broadcast_to(row, (16, 128)).astype(bf16)


def row_of(columns):
    lane = lax.broadcasted_iota(jnp.int32, (32, 128), 1)
    token = lax.broadcasted_iota(jnp.int32, (32, 128), 0)
    spreaded = jnp.zeros((32, 128), f32)
    for k, column in enumerate(columns):
        spreaded = jnp.where(lane == token + 32 * k, column, spreaded)
    return jnp.sum(spreaded, axis=0, keepdims=True)


def column_of(row):
    lane = lax.broadcasted_iota(jnp.int32, (32, 128), 1)
    token = lax.broadcasted_iota(jnp.int32, (32, 128), 0)
    return jnp.sum(jnp.where(lane == token, row, 0.0), axis=1, keepdims=True)


def column(ref):
    row = ref[...].astype(f32).reshape(1, 32)
    lane = lax.broadcasted_iota(jnp.int32, (32, 32), 1)
    token = lax.broadcasted_iota(jnp.int32, (32, 32), 0)
    return jnp.sum(jnp.where(lane == token, row, 0.0), axis=1, keepdims=True)


def stats_kernel(
    first_ref, got_ref, targets_ref, weight_ref, logits_ref, scale_ref, stats_ref, mark_ref
):
    at = column(targets_ref).astype(jnp.int32) - first_ref[0]
    mark = (lax.broadcasted_iota(jnp.int32, (32, 512), 1) == at).astype(f32)
    total = jnp.zeros((144, 128), f32)
    for k in range(16):
        total = total + got_ref[k].astype(f32)
    lane = lax.broadcasted_iota(jnp.int32, (32, 128), 1)
    token = lax.broadcasted_iota(jnp.int32, (32, 128), 0)
    held = (lax.rem(lane, 32) == token) & (lane < 96)
    squares = jnp.sum(jnp.where(held, total[128:129], 0.0), axis=1, keepdims=True)
    inv = lax.rsqrt(squares / D + EPSILON)
    logits = jnp.concatenate([total[32 * j : 32 * j + 32] for j in range(4)], axis=1) * inv
    top = jnp.max(logits, axis=1, keepdims=True)
    e = jnp.exp(logits - top)
    row = row_of(
        [
            top,
            jnp.sum(e, axis=1, keepdims=True),
            jnp.sum(e * logits, axis=1, keepdims=True),
            jnp.sum(logits * mark, axis=1, keepdims=True),
        ]
    )
    logits_ref[...] = logits
    scale_ref[...] = columns_of([inv, column(weight_ref)], 128)
    mark_ref[...] = mark
    stats_ref[...] = jnp.broadcast_to(row[None], (32, 1, 128))


def dlogits_kernel(stats_ref, logits_ref, scale_ref, mark_ref, gate_ref, up_ref, out_ref):
    gate, up = gate_ref[...].astype(f32), up_ref[...].astype(f32)
    hidden = (gate * jax.nn.sigmoid(gate) * up).astype(bf16)
    stats = stats_ref[...].reshape(32, 128)
    lane = lax.broadcasted_iota(jnp.int32, (32, 128), 1)
    top = jnp.max(stats, axis=0, keepdims=True)
    scale = jnp.exp(jnp.where(lane < 32, stats - top, 0.0))
    sums = pltpu.roll(stats, 96, 1)
    means = pltpu.roll(stats, 64, 1)
    picked = pltpu.roll(stats, 32, 1)
    total = jnp.sum(sums * scale, axis=0, keepdims=True)
    mean = jnp.sum(means * scale, axis=0, keepdims=True) / total
    inner = mean - jnp.sum(picked, axis=0, keepdims=True)
    weight = scale_ref[:, 1:2]
    top, total, inner = column_of(top), column_of(total), column_of(inner) * weight / D
    probability = jnp.exp(logits_ref[...] - top) / total
    dlogits = ((probability - mark_ref[...]) * weight).astype(bf16)
    tail = columns_of(thirds(scale_ref[:, :1]) + thirds(inner), 64).astype(bf16)
    for k in range(8):
        out_ref[k, :, :512] = dlogits
        out_ref[k, :, 512:960] = hidden
        out_ref[k, :, 960:] = tail


def half_rows(core_ref, side, mine_ref, others_ref, lanes):
    here = core_ref[0] == side
    return jnp.concatenate(
        [
            jnp.where(here, mine_ref[f, y : y + 16, lanes], others_ref[f, y : y + 16, lanes])
            for y in (0, 16)
            for f in range(FARS)
        ]
    )


def back_kernel(core_ref, mine_ref, others_ref, weight_ref, out_ref):
    for side in range(2):
        rows = half_rows(core_ref, side, mine_ref, others_ref, slice(0, 512))
        part = jnp.dot(rows, weight_ref[...], preferred_element_type=f32)
        out_ref[2 * side] = part[:128].astype(bf16)
        out_ref[2 * side + 1] = part[128:].astype(bf16)


def weights_kernel(
    core_ref, mine_ref, others_ref, x_ref, gain_ref, rows_ref, head_ref, down_ref, sum_ref
):
    def add(ref, side, part):
        ref[...] = part if side == 0 else ref[...] + part

    def product(a, b):
        return lax.dot_general(a, b, (((0,), (0,)), ((), ())), preferred_element_type=f32)

    gain = gain_ref[...].reshape(1, 768)
    for side in range(2):
        got = half_rows(core_ref, side, mine_ref, others_ref, slice(0, 1024))
        tail = got[:, 896:].astype(f32)
        inv = tail[:, 64:65] + tail[:, 65:66] + tail[:, 66:67]
        inner = tail[:, 67:68] + tail[:, 68:69] + tail[:, 69:70]
        unit_rows = x_ref[2 * side : 2 * side + 2].reshape(256, 768).astype(f32) * inv
        add(head_ref, side, product(got[:, :512], (unit_rows * gain).astype(bf16)))
        rows = rows_ref[2 * side : 2 * side + 2].reshape(256, 768)
        add(down_ref, side, product(got[:, 512:960], rows))
        scaled = rows.astype(f32) * (1.0 / inv) + unit_rows * inner
        add(sum_ref, side, jnp.sum(scaled * unit_rows, axis=0, keepdims=True))
    sum_ref[...] = sum_ref[...] / gain


def grad_kernel(
    core_ref, near_ref, far_ref, low_ref, got_ref, mine_ref, others_ref, x_ref, gain_ref,
    out_ref,
):
    rows = pl.ds(pl.multiple_of(low_ref[0] * 16, 16), 16)
    here = core_ref[0] == near_ref[0]
    tail = jnp.where(
        here, mine_ref[far_ref[0], rows, 896:], others_ref[far_ref[0], rows, 896:]
    ).astype(f32)
    inv = tail[:, 64:65] + tail[:, 65:66] + tail[:, 66:67]
    inner = tail[:, 67:68] + tail[:, 68:69] + tail[:, 69:70]
    normed_back = jnp.zeros((16, 768), f32)
    for k in range(FARS):
        normed_back = normed_back + got_ref[k].astype(f32)
    unit_rows = x_ref[...].astype(f32) * inv
    grad = (inv * (normed_back * gain_ref[...].reshape(1, 768) - unit_rows * inner)).astype(bf16)
    for k in range(FARS):
        out_ref[k] = grad


def hidden_back_kernel(rows_ref, weight_ref, out_ref, held, sems):
    copies = []
    for half in range(2):
        rows = pl.ds(256 * half, 256)
        part = lax.dot_general(
            token_rows(rows_ref, 4 * half, 4),
            weight_ref[...],
            (((1,), (1,)), ((), ())),
            preferred_element_type=f32,
        )
        held[rows, :] = part.astype(bf16)
        copies.append(pltpu.make_async_copy(held.at[rows], out_ref.at[rows], sems.at[half]))
        copies[-1].start()
    for copy in copies:
        copy.wait()


def hidden_back(rows, weight):
    shape, whole = (512, 448), pl.BlockSpec(memory_space=pltpu.VMEM)
    return pl.pallas_call(
        hidden_back_kernel,
        out_shape=jax.ShapeDtypeStruct(shape, bf16),
        in_specs=[whole, whole],
        out_specs=pl.BlockSpec(memory_space=pl.ANY),
        scratch_shapes=[pltpu.VMEM(shape, bf16), pltpu.SemaphoreType.DMA((2,))],
        compiler_params=pltpu.CompilerParams(vmem_limit_bytes=16 << 20),
        cost_estimate=pl.CostEstimate(
            flops=2 * 512 * 448 * 768, bytes_accessed=2 << 20, transcendentals=0
        ),
    )(rows, weight)


def per_device(
    stream, norm_gain, head_weight, down_weight, gate_pre, up_pre, targets, token_weight
):
    vocab_local = head_weight.shape[0]
    t = lax.axis_index(TENSOR)
    first = (t * vocab_local).astype(jnp.int32)[None]
    places = [lax.axis_index(a).astype(jnp.int32)[None] for a in ("c", "zn", "zf", "yl")]
    rows, first, places = lax.optimization_barrier((stream, first, places))
    core = places[0]
    far = spread(rows, FAR, FARS)
    x_blocks = spread(far, NEAR, NEARS)
    part = on_core(
        logits_kernel,
        [((16, 144, 128), bf16)],
        x_blocks.reshape(NEARS, FARS * 16, 768),
        norm_gain,
        head_weight,
        flops=2 * 512 * 512 * 768,
    )[0]
    got = exchange(part, DP)
    logits, scale, stats, mark = on_core(
        stats_kernel,
        [((32, 512), f32), ((32, 128), f32), ((32, 1, 128), f32), ((32, 512), f32)],
        first,
        got,
        targets,
        token_weight,
    )
    stats = exchange(stats, TENSOR)
    sent = on_core(
        dlogits_kernel, [((8, 32, 1024), bf16)], stats, logits, scale, mark, gate_pre, up_pre
    )[0]
    mine = exchange(sent, CHIPS)
    others = other_core(mine)

    back = on_core(
        back_kernel,
        [((NEARS, FARS * 16, 768), bf16)],
        core,
        mine,
        others,
        head_weight,
        flops=2 * 512 * 512 * 768,
    )[0]
    near = jnp.sum(exchange(back, NEAR).astype(f32), axis=0).astype(bf16)
    got = exchange(near.reshape(FARS, 16, 768), FAR)
    sent = on_core(
        grad_kernel,
        [((FARS, 16, 768), bf16)],
        *places,
        got,
        mine,
        others,
        stream,
        norm_gain,
    )[0]
    gathered = spread(exchange(sent, FAR).reshape(FARS * 16, 768), NEAR, NEARS)
    hidden_part = hidden_back(gathered, down_weight)
    gathered, sent, x_blocks, mine, others, hidden_part = lax.optimization_barrier(
        (gathered, sent, x_blocks, mine, others, hidden_part)
    )
    stream_grad = sent[0]
    head_grad, down_grad, gain_grad = on_core(
        weights_kernel,
        [((512, 768), f32), ((448, 768), f32), ((1, 768), f32)],
        core,
        mine,
        others,
        x_blocks.reshape(NEARS, FARS * 16, 768),
        norm_gain,
        gathered,
        flops=2 * 512 * 960 * 768,
    )
    hidden_grad = jnp.sum(exchange(hidden_part.reshape(16, 32, 448), DP).astype(f32), axis=0)
    gate_float = gate_pre.astype(f32)
    up_float = up_pre.astype(f32)
    sigmoid_gate = jax.nn.sigmoid(gate_float)
    up_grad = (hidden_grad * gate_float * sigmoid_gate).astype(bf16)
    gate_grad = (
        hidden_grad * up_float * sigmoid_gate * (1.0 + gate_float * (1.0 - sigmoid_gate))
    ).astype(bf16)
    return (head_grad, down_grad, stream_grad, gain_grad[0], gate_grad, up_grad)


def solution(mesh):
    fine = Mesh(mesh.devices.reshape(8, 2, 2, 2, 4, 2), ("zf", "zn", "yl", "yh", "x", "c"))
    return jax.shard_map(
        per_device,
        mesh=fine,
        in_specs=(
            P(TENSOR, DP),
            P(DP),
            P(TENSOR, DP),
            P(TENSOR, DP),
            P(DP, TENSOR),
            P(DP, TENSOR),
            P(DP),
            P(DP),
        ),
        out_specs=(
            P(TENSOR, DP),
            P(TENSOR, DP),
            P(TENSOR, DP),
            P(DP),
            P(DP, TENSOR),
            P(DP, TENSOR),
        ),
        check_vma=False,
    )
```

```python
import jax
import jax.numpy as jnp
from jax import lax
from jax.experimental import pallas as pl
from jax.experimental.pallas import tpu as pltpu
from jax.sharding import Mesh, PartitionSpec as P

D = 12288
EPSILON = 1e-05
TENSOR = ("z3", "z2", "z1", "z0", "yl")
DP = ("yh", "x1", "x0", "c")
FAR, NEAR = ("z1", "z3", "z2"), ("z0", "yl")
CHIPS = ("x0", "yh", "x1")
DEVICES = CHIPS + ("c",)
FARS, NEARS = 8, 4
f32, bf16 = jnp.float32, jnp.bfloat16


def on_core(kernel, outs, *args, flops=0):
    whole = pl.BlockSpec(memory_space=pltpu.VMEM)
    outs = [jax.ShapeDtypeStruct(s, d) for s, d in outs]
    moved = sum(a.size * a.dtype.itemsize for a in list(args) + outs)
    return pl.pallas_call(
        kernel,
        out_shape=outs,
        in_specs=[
            pl.BlockSpec(memory_space=pltpu.SMEM) if a.shape == (1,) else whole for a in args
        ],
        out_specs=[whole] * len(outs),
        compiler_params=pltpu.CompilerParams(vmem_limit_bytes=16 << 20),
        cost_estimate=pl.CostEstimate(flops=flops, bytes_accessed=moved, transcendentals=0),
    )(*args)


def exchange(blocks, axes):
    return lax.all_to_all(blocks, axes, 0, 0, tiled=True)


def spread(block, axes, n):
    return exchange(jnp.broadcast_to(block[None], (n,) + block.shape), axes)


def other_core(block):
    return lax.ppermute(block, "c", [(0, 1), (1, 0)])


def token_rows(ref, first, count):
    return jnp.concatenate(
        [ref[n, f * 16 : f * 16 + 16] for f in range(first, first + count) for n in range(NEARS)]
    )


def columns_of(parts, width):
    lane = lax.broadcasted_iota(jnp.int32, (parts[0].shape[0], width), 1)
    out = jnp.zeros((parts[0].shape[0], width), f32)
    for k, part in enumerate(parts):
        out = jnp.where(lane == k, part, out)
    return out


def thirds(v):
    hi = v.astype(bf16).astype(f32)
    mid = (v - hi).astype(bf16).astype(f32)
    return [hi, mid, v - hi - mid]


def logits_kernel(x_ref, gain_ref, weight_ref, out_ref):
    gain = gain_ref[...].reshape(1, 768)
    for half in range(2):
        x = token_rows(x_ref, 4 * half, 4).astype(f32)
        scaled = (x * gain).astype(bf16)
        part = lax.dot_general(
            scaled, weight_ref[...], (((1,), (1,)), ((), ())), preferred_element_type=f32
        )
        part = part.astype(bf16)
        squares = jnp.sum(x * x, axis=1, keepdims=True)
        for k in range(8):
            to, rows = 8 * half + k, slice(32 * k, 32 * k + 32)
            for j in range(4):
                out_ref[to, 32 * j : 32 * j + 32, :] = part[rows, 128 * j : 128 * j + 128]
            row = row_of(thirds(squares[rows]))
            out_ref[to, 128:, :] = jnp.broadcast_to(row, (16, 128)).astype(bf16)


def row_of(columns):
    lane = lax.broadcasted_iota(jnp.int32, (32, 128), 1)
    token = lax.broadcasted_iota(jnp.int32, (32, 128), 0)
    spreaded = jnp.zeros((32, 128), f32)
    for k, column in enumerate(columns):
        spreaded = jnp.where(lane == token + 32 * k, column, spreaded)
    return jnp.sum(spreaded, axis=0, keepdims=True)


def column_of(row):
    lane = lax.broadcasted_iota(jnp.int32, (32, 128), 1)
    token = lax.broadcasted_iota(jnp.int32, (32, 128), 0)
    return jnp.sum(jnp.where(lane == token, row, 0.0), axis=1, keepdims=True)


def column(ref):
    row = ref[...].astype(f32).reshape(1, 32)
    lane = lax.broadcasted_iota(jnp.int32, (32, 32), 1)
    token = lax.broadcasted_iota(jnp.int32, (32, 32), 0)
    return jnp.sum(jnp.where(lane == token, row, 0.0), axis=1, keepdims=True)


def stats_kernel(
    first_ref, got_ref, targets_ref, weight_ref, logits_ref, scale_ref, stats_ref, mark_ref
):
    at = column(targets_ref).astype(jnp.int32) - first_ref[0]
    mark = (lax.broadcasted_iota(jnp.int32, (32, 512), 1) == at).astype(f32)
    total = jnp.zeros((144, 128), f32)
    for k in range(16):
        total = total + got_ref[k].astype(f32)
    lane = lax.broadcasted_iota(jnp.int32, (32, 128), 1)
    token = lax.broadcasted_iota(jnp.int32, (32, 128), 0)
    held = (lax.rem(lane, 32) == token) & (lane < 96)
    squares = jnp.sum(jnp.where(held, total[128:129], 0.0), axis=1, keepdims=True)
    inv = lax.rsqrt(squares / D + EPSILON)
    logits = jnp.concatenate([total[32 * j : 32 * j + 32] for j in range(4)], axis=1) * inv
    top = jnp.max(logits, axis=1, keepdims=True)
    e = jnp.exp(logits - top)
    row = row_of(
        [
            top,
            jnp.sum(e, axis=1, keepdims=True),
            jnp.sum(e * logits, axis=1, keepdims=True),
            jnp.sum(logits * mark, axis=1, keepdims=True),
        ]
    )
    logits_ref[...] = logits
    scale_ref[...] = columns_of([inv, column(weight_ref)], 128)
    mark_ref[...] = mark
    stats_ref[...] = jnp.broadcast_to(row[None], (32, 1, 128))


def dlogits_kernel(stats_ref, logits_ref, scale_ref, mark_ref, gate_ref, up_ref, out_ref):
    gate, up = gate_ref[...].astype(f32), up_ref[...].astype(f32)
    hidden = (gate * jax.nn.sigmoid(gate) * up).astype(bf16)
    stats = stats_ref[...].reshape(32, 128)
    lane = lax.broadcasted_iota(jnp.int32, (32, 128), 1)
    top = jnp.max(stats, axis=0, keepdims=True)
    scale = jnp.exp(jnp.where(lane < 32, stats - top, 0.0))
    sums = pltpu.roll(stats, 96, 1)
    means = pltpu.roll(stats, 64, 1)
    picked = pltpu.roll(stats, 32, 1)
    total = jnp.sum(sums * scale, axis=0, keepdims=True)
    mean = jnp.sum(means * scale, axis=0, keepdims=True) / total
    inner = mean - jnp.sum(picked, axis=0, keepdims=True)
    weight = scale_ref[:, 1:2]
    top, total, inner = column_of(top), column_of(total), column_of(inner) * weight / D
    probability = jnp.exp(logits_ref[...] - top) / total
    dlogits = ((probability - mark_ref[...]) * weight).astype(bf16)
    tail = columns_of(thirds(scale_ref[:, :1]) + thirds(inner), 64).astype(bf16)
    for k in range(8):
        out_ref[k, :, :512] = dlogits
        out_ref[k, :, 512:960] = hidden
        out_ref[k, :, 960:] = tail


def half_rows(core_ref, side, mine_ref, others_ref, lanes):
    here = core_ref[0] == side
    return jnp.concatenate(
        [
            jnp.where(here, mine_ref[f, y : y + 16, lanes], others_ref[f, y : y + 16, lanes])
            for y in (0, 16)
            for f in range(FARS)
        ]
    )


def back_kernel(core_ref, mine_ref, others_ref, weight_ref, out_ref):
    for side in range(2):
        rows = half_rows(core_ref, side, mine_ref, others_ref, slice(0, 512))
        part = jnp.dot(rows, weight_ref[...], preferred_element_type=f32)
        out_ref[2 * side] = part[:128].astype(bf16)
        out_ref[2 * side + 1] = part[128:].astype(bf16)


def weights_kernel(
    core_ref, mine_ref, others_ref, x_ref, gain_ref, rows_ref, head_ref, down_ref, sum_ref
):
    def add(ref, side, part):
        ref[...] = part if side == 0 else ref[...] + part

    def product(a, b):
        return lax.dot_general(a, b, (((0,), (0,)), ((), ())), preferred_element_type=f32)

    gain = gain_ref[...].reshape(1, 768)
    for side in range(2):
        got = half_rows(core_ref, side, mine_ref, others_ref, slice(0, 1024))
        tail = got[:, 896:].astype(f32)
        inv = tail[:, 64:65] + tail[:, 65:66] + tail[:, 66:67]
        inner = tail[:, 67:68] + tail[:, 68:69] + tail[:, 69:70]
        unit_rows = x_ref[2 * side : 2 * side + 2].reshape(256, 768).astype(f32) * inv
        add(head_ref, side, product(got[:, :512], (unit_rows * gain).astype(bf16)))
        rows = rows_ref[2 * side : 2 * side + 2].reshape(256, 768)
        add(down_ref, side, product(got[:, 512:960], rows))
        scaled = rows.astype(f32) * (1.0 / inv) + unit_rows * inner
        add(sum_ref, side, jnp.sum(scaled * unit_rows, axis=0, keepdims=True))
    sum_ref[...] = sum_ref[...] / gain


def grad_kernel(
    core_ref, near_ref, far_ref, low_ref, got_ref, mine_ref, others_ref, x_ref, gain_ref,
    out_ref,
):
    rows = pl.ds(pl.multiple_of(low_ref[0] * 16, 16), 16)
    here = core_ref[0] == near_ref[0]
    tail = jnp.where(
        here, mine_ref[far_ref[0], rows, 896:], others_ref[far_ref[0], rows, 896:]
    ).astype(f32)
    inv = tail[:, 64:65] + tail[:, 65:66] + tail[:, 66:67]
    inner = tail[:, 67:68] + tail[:, 68:69] + tail[:, 69:70]
    normed_back = jnp.zeros((16, 768), f32)
    for k in range(FARS):
        normed_back = normed_back + got_ref[k].astype(f32)
    unit_rows = x_ref[...].astype(f32) * inv
    grad = (inv * (normed_back * gain_ref[...].reshape(1, 768) - unit_rows * inner)).astype(bf16)
    for k in range(FARS):
        out_ref[k] = grad


def hidden_back_kernel(rows_ref, weight_ref, out_ref, held, sems):
    copies = []
    for half in range(2):
        rows = pl.ds(256 * half, 256)
        part = lax.dot_general(
            token_rows(rows_ref, 4 * half, 4),
            weight_ref[...],
            (((1,), (1,)), ((), ())),
            preferred_element_type=f32,
        )
        held[rows, :] = part.astype(bf16)
        copies.append(pltpu.make_async_copy(held.at[rows], out_ref.at[rows], sems.at[half]))
        copies[-1].start()
    for copy in copies:
        copy.wait()


def hidden_back(rows, weight):
    shape, whole = (512, 448), pl.BlockSpec(memory_space=pltpu.VMEM)
    return pl.pallas_call(
        hidden_back_kernel,
        out_shape=jax.ShapeDtypeStruct(shape, bf16),
        in_specs=[whole, whole],
        out_specs=pl.BlockSpec(memory_space=pl.ANY),
        scratch_shapes=[pltpu.VMEM(shape, bf16), pltpu.SemaphoreType.DMA((2,))],
        compiler_params=pltpu.CompilerParams(vmem_limit_bytes=16 << 20),
        cost_estimate=pl.CostEstimate(
            flops=2 * 512 * 448 * 768, bytes_accessed=2 << 20, transcendentals=0
        ),
    )(rows, weight)


def per_device(
    stream, norm_gain, head_weight, down_weight, gate_pre, up_pre, targets, token_weight
):
    vocab_local = head_weight.shape[0]
    t = lax.axis_index(TENSOR)
    first = (t * vocab_local).astype(jnp.int32)[None]
    places = [lax.axis_index(a).astype(jnp.int32)[None] for a in ("c", "z0", FAR, "yl")]
    rows, first, places = lax.optimization_barrier((stream, first, places))
    core = places[0]
    far = spread(rows, FAR, FARS)
    x_blocks = spread(far, NEAR, NEARS)
    part = on_core(
        logits_kernel,
        [((16, 144, 128), bf16)],
        x_blocks.reshape(NEARS, FARS * 16, 768),
        norm_gain,
        head_weight,
        flops=2 * 512 * 512 * 768,
    )[0]
    got = exchange(part, DEVICES)
    logits, scale, stats, mark = on_core(
        stats_kernel,
        [((32, 512), f32), ((32, 128), f32), ((32, 1, 128), f32), ((32, 512), f32)],
        first,
        got,
        targets,
        token_weight,
    )
    stats = exchange(stats, TENSOR[::-1])
    sent = on_core(
        dlogits_kernel, [((8, 32, 1024), bf16)], stats, logits, scale, mark, gate_pre, up_pre
    )[0]
    mine = exchange(sent, CHIPS)
    others = other_core(mine)

    back = on_core(
        back_kernel,
        [((NEARS, FARS * 16, 768), bf16)],
        core,
        mine,
        others,
        head_weight,
        flops=2 * 512 * 512 * 768,
    )[0]
    near = jnp.sum(exchange(back, NEAR).astype(f32), axis=0).astype(bf16)
    got = exchange(near.reshape(FARS, 16, 768), FAR)
    sent = on_core(
        grad_kernel,
        [((FARS, 16, 768), bf16)],
        *places,
        got,
        mine,
        others,
        stream,
        norm_gain,
    )[0]
    gathered = spread(exchange(sent, FAR).reshape(FARS * 16, 768), NEAR, NEARS)
    hidden_part = hidden_back(gathered, down_weight)
    gathered, sent, x_blocks, mine, others, hidden_part = lax.optimization_barrier(
        (gathered, sent, x_blocks, mine, others, hidden_part)
    )
    stream_grad = sent[0]
    head_grad, down_grad, gain_grad = on_core(
        weights_kernel,
        [((512, 768), f32), ((448, 768), f32), ((1, 768), f32)],
        core,
        mine,
        others,
        x_blocks.reshape(NEARS, FARS * 16, 768),
        norm_gain,
        gathered,
        flops=2 * 512 * 960 * 768,
    )
    hidden_grad = jnp.sum(exchange(hidden_part.reshape(16, 32, 448), DEVICES).astype(f32), axis=0)
    gate_float = gate_pre.astype(f32)
    up_float = up_pre.astype(f32)
    sigmoid_gate = jax.nn.sigmoid(gate_float)
    up_grad = (hidden_grad * gate_float * sigmoid_gate).astype(bf16)
    gate_grad = (
        hidden_grad * up_float * sigmoid_gate * (1.0 + gate_float * (1.0 - sigmoid_gate))
    ).astype(bf16)
    return (head_grad, down_grad, stream_grad, gain_grad[0], gate_grad, up_grad)


def solution(mesh):
    fine = Mesh(mesh.devices.reshape((2,) * 9), TENSOR + DP)
    return jax.shard_map(
        per_device,
        mesh=fine,
        in_specs=(
            P(TENSOR, DP),
            P(DP),
            P(TENSOR, DP),
            P(TENSOR, DP),
            P(DP, TENSOR),
            P(DP, TENSOR),
            P(DP),
            P(DP),
        ),
        out_specs=(
            P(TENSOR, DP),
            P(TENSOR, DP),
            P(TENSOR, DP),
            P(DP),
            P(DP, TENSOR),
            P(DP, TENSOR),
        ),
        check_vma=False,
    )
```

```python
import jax
import jax.numpy as jnp
from jax import lax
from jax.experimental import pallas as pl
from jax.experimental.pallas import tpu as pltpu
from jax.sharding import Mesh, PartitionSpec as P

D = 12288
EPSILON = 1e-05
TENSOR = ("z3", "z2", "z1", "z0", "yl")
DP = ("yh", "x1", "x0", "c")
FAR, NEAR = ("z1", "z3", "z2"), ("z0", "yl")
CHIPS = ("x0", "yh", "x1")
DEVICES = CHIPS + ("c",)
FARS, NEARS = 8, 4
f32, bf16 = jnp.float32, jnp.bfloat16


def on_core(kernel, outs, *args, flops=0):
    whole = pl.BlockSpec(memory_space=pltpu.VMEM)
    outs = [jax.ShapeDtypeStruct(s, d) for s, d in outs]
    moved = sum(a.size * a.dtype.itemsize for a in list(args) + outs)
    return pl.pallas_call(
        kernel,
        out_shape=outs,
        in_specs=[
            pl.BlockSpec(memory_space=pltpu.SMEM) if a.shape == (1,) else whole for a in args
        ],
        out_specs=[whole] * len(outs),
        compiler_params=pltpu.CompilerParams(vmem_limit_bytes=16 << 20),
        cost_estimate=pl.CostEstimate(flops=flops, bytes_accessed=moved, transcendentals=0),
    )(*args)


def exchange(blocks, axes):
    return lax.all_to_all(blocks, axes, 0, 0, tiled=True)


def spread(block, axes, n):
    return exchange(jnp.broadcast_to(block[None], (n,) + block.shape), axes)


def other_core(block):
    return lax.ppermute(block, "c", [(0, 1), (1, 0)])


def token_rows(ref, first, count):
    return jnp.concatenate(
        [ref[n, f * 16 : f * 16 + 16] for f in range(first, first + count) for n in range(NEARS)]
    )


def columns_of(parts, width):
    lane = lax.broadcasted_iota(jnp.int32, (parts[0].shape[0], width), 1)
    out = jnp.zeros((parts[0].shape[0], width), f32)
    for k, part in enumerate(parts):
        out = jnp.where(lane == k, part, out)
    return out


def thirds(v):
    hi = v.astype(bf16).astype(f32)
    mid = (v - hi).astype(bf16).astype(f32)
    return [hi, mid, v - hi - mid]


def logits_kernel(x_ref, gain_ref, weight_ref, out_ref):
    gain = gain_ref[...].reshape(1, 768)
    for half in range(2):
        x = token_rows(x_ref, 4 * half, 4).astype(f32)
        scaled = (x * gain).astype(bf16)
        part = lax.dot_general(
            scaled, weight_ref[...], (((1,), (1,)), ((), ())), preferred_element_type=f32
        )
        part = part.astype(bf16)
        squares = jnp.sum(x * x, axis=1, keepdims=True)
        for k in range(8):
            to, rows = 8 * half + k, slice(32 * k, 32 * k + 32)
            for j in range(4):
                out_ref[to, 32 * j : 32 * j + 32, :] = part[rows, 128 * j : 128 * j + 128]
            row = row_of(thirds(squares[rows]))
            out_ref[to, 128:, :] = jnp.broadcast_to(row, (16, 128)).astype(bf16)


def row_of(columns):
    lane = lax.broadcasted_iota(jnp.int32, (32, 128), 1)
    token = lax.broadcasted_iota(jnp.int32, (32, 128), 0)
    spreaded = jnp.zeros((32, 128), f32)
    for k, column in enumerate(columns):
        spreaded = jnp.where(lane == token + 32 * k, column, spreaded)
    return jnp.sum(spreaded, axis=0, keepdims=True)


def column_of(row):
    lane = lax.broadcasted_iota(jnp.int32, (32, 128), 1)
    token = lax.broadcasted_iota(jnp.int32, (32, 128), 0)
    return jnp.sum(jnp.where(lane == token, row, 0.0), axis=1, keepdims=True)


def column(ref):
    row = ref[...].astype(f32).reshape(1, 32)
    lane = lax.broadcasted_iota(jnp.int32, (32, 32), 1)
    token = lax.broadcasted_iota(jnp.int32, (32, 32), 0)
    return jnp.sum(jnp.where(lane == token, row, 0.0), axis=1, keepdims=True)


def stats_kernel(
    first_ref, got_ref, targets_ref, weight_ref, logits_ref, scale_ref, stats_ref, mark_ref
):
    at = column(targets_ref).astype(jnp.int32) - first_ref[0]
    mark = (lax.broadcasted_iota(jnp.int32, (32, 512), 1) == at).astype(f32)
    total = jnp.zeros((144, 128), f32)
    for k in range(16):
        total = total + got_ref[k].astype(f32)
    lane = lax.broadcasted_iota(jnp.int32, (32, 128), 1)
    token = lax.broadcasted_iota(jnp.int32, (32, 128), 0)
    held = (lax.rem(lane, 32) == token) & (lane < 96)
    squares = jnp.sum(jnp.where(held, total[128:129], 0.0), axis=1, keepdims=True)
    inv = lax.rsqrt(squares / D + EPSILON)
    logits = jnp.concatenate([total[32 * j : 32 * j + 32] for j in range(4)], axis=1) * inv
    top = jnp.max(logits, axis=1, keepdims=True)
    e = jnp.exp(logits - top)
    row = row_of(
        [
            top,
            jnp.sum(e, axis=1, keepdims=True),
            jnp.sum(e * logits, axis=1, keepdims=True),
            jnp.sum(logits * mark, axis=1, keepdims=True),
        ]
    )
    logits_ref[...] = logits
    scale_ref[...] = columns_of([inv, column(weight_ref)], 128)
    mark_ref[...] = mark
    stats_ref[...] = jnp.broadcast_to(row[None], (32, 1, 128))


def dlogits_kernel(stats_ref, logits_ref, scale_ref, mark_ref, gate_ref, up_ref, out_ref):
    gate, up = gate_ref[...].astype(f32), up_ref[...].astype(f32)
    hidden = (gate * jax.nn.sigmoid(gate) * up).astype(bf16)
    stats = stats_ref[...].reshape(32, 128)
    lane = lax.broadcasted_iota(jnp.int32, (32, 128), 1)
    top = jnp.max(stats, axis=0, keepdims=True)
    scale = jnp.exp(jnp.where(lane < 32, stats - top, 0.0))
    sums = pltpu.roll(stats, 96, 1)
    means = pltpu.roll(stats, 64, 1)
    picked = pltpu.roll(stats, 32, 1)
    total = jnp.sum(sums * scale, axis=0, keepdims=True)
    mean = jnp.sum(means * scale, axis=0, keepdims=True) / total
    inner = mean - jnp.sum(picked, axis=0, keepdims=True)
    weight = scale_ref[:, 1:2]
    top, total, inner = column_of(top), column_of(total), column_of(inner) * weight / D
    probability = jnp.exp(logits_ref[...] - top) / total
    dlogits = ((probability - mark_ref[...]) * weight).astype(bf16)
    tail = columns_of(thirds(scale_ref[:, :1]) + thirds(inner), 64).astype(bf16)
    for k in range(8):
        out_ref[k, :, :512] = dlogits
        out_ref[k, :, 512:960] = hidden
        out_ref[k, :, 960:] = tail


def half_rows(core_ref, side, mine_ref, others_ref, lanes):
    here = core_ref[0] == side
    return jnp.concatenate(
        [
            jnp.where(here, mine_ref[f, y : y + 16, lanes], others_ref[f, y : y + 16, lanes])
            for y in (0, 16)
            for f in range(FARS)
        ]
    )


def back_kernel(core_ref, mine_ref, others_ref, weight_ref, out_ref):
    for side in range(2):
        rows = half_rows(core_ref, side, mine_ref, others_ref, slice(0, 512))
        part = jnp.dot(rows, weight_ref[...], preferred_element_type=f32)
        out_ref[2 * side] = part[:128].astype(bf16)
        out_ref[2 * side + 1] = part[128:].astype(bf16)


def weights_kernel(
    core_ref, mine_ref, others_ref, x_ref, gain_ref, rows_ref, head_ref, down_ref, sum_ref
):
    def add(ref, side, part):
        ref[...] = part if side == 0 else ref[...] + part

    def product(a, b):
        return lax.dot_general(a, b, (((0,), (0,)), ((), ())), preferred_element_type=f32)

    gain = gain_ref[...].reshape(1, 768)
    for side in range(2):
        got = half_rows(core_ref, side, mine_ref, others_ref, slice(0, 1024))
        tail = got[:, 896:].astype(f32)
        inv = tail[:, 64:65] + tail[:, 65:66] + tail[:, 66:67]
        inner = tail[:, 67:68] + tail[:, 68:69] + tail[:, 69:70]
        unit_rows = x_ref[2 * side : 2 * side + 2].reshape(256, 768).astype(f32) * inv
        add(head_ref, side, product(got[:, :512], (unit_rows * gain).astype(bf16)))
        rows = rows_ref[2 * side : 2 * side + 2].reshape(256, 768)
        add(down_ref, side, product(got[:, 512:960], rows))
        scaled = rows.astype(f32) * (1.0 / inv) + unit_rows * inner
        add(sum_ref, side, jnp.sum(scaled * unit_rows, axis=0, keepdims=True))
    sum_ref[...] = sum_ref[...] / gain


def grad_kernel(
    core_ref, near_ref, far_ref, low_ref, got_ref, mine_ref, others_ref, x_ref, gain_ref,
    out_ref,
):
    rows = pl.ds(pl.multiple_of(low_ref[0] * 16, 16), 16)
    here = core_ref[0] == near_ref[0]
    tail = jnp.where(
        here, mine_ref[far_ref[0], rows, 896:], others_ref[far_ref[0], rows, 896:]
    ).astype(f32)
    inv = tail[:, 64:65] + tail[:, 65:66] + tail[:, 66:67]
    inner = tail[:, 67:68] + tail[:, 68:69] + tail[:, 69:70]
    normed_back = jnp.zeros((16, 768), f32)
    for k in range(FARS):
        normed_back = normed_back + got_ref[k].astype(f32)
    unit_rows = x_ref[...].astype(f32) * inv
    grad = (inv * (normed_back * gain_ref[...].reshape(1, 768) - unit_rows * inner)).astype(bf16)
    for k in range(FARS):
        out_ref[k] = grad


def hidden_back_kernel(rows_ref, weight_ref, out_ref, held, sems):
    copies = []
    for half in range(2):
        rows = pl.ds(256 * half, 256)
        part = lax.dot_general(
            token_rows(rows_ref, 4 * half, 4),
            weight_ref[...],
            (((1,), (1,)), ((), ())),
            preferred_element_type=f32,
        )
        held[rows, :] = part.astype(bf16)
        copies.append(pltpu.make_async_copy(held.at[rows], out_ref.at[rows], sems.at[half]))
        copies[-1].start()
    for copy in copies:
        copy.wait()


def hidden_back(rows, weight):
    shape, whole = (512, 448), pl.BlockSpec(memory_space=pltpu.VMEM)
    return pl.pallas_call(
        hidden_back_kernel,
        out_shape=jax.ShapeDtypeStruct(shape, bf16),
        in_specs=[whole, whole],
        out_specs=pl.BlockSpec(memory_space=pl.ANY),
        scratch_shapes=[pltpu.VMEM(shape, bf16), pltpu.SemaphoreType.DMA((2,))],
        compiler_params=pltpu.CompilerParams(vmem_limit_bytes=16 << 20),
        cost_estimate=pl.CostEstimate(
            flops=2 * 512 * 448 * 768, bytes_accessed=2 << 20, transcendentals=0
        ),
    )(rows, weight)


def per_device(
    stream, norm_gain, head_weight, down_weight, gate_pre, up_pre, targets, token_weight
):
    vocab_local = head_weight.shape[0]
    t = lax.axis_index(TENSOR)
    first = (t * vocab_local).astype(jnp.int32)[None]
    places = [lax.axis_index(a).astype(jnp.int32)[None] for a in ("c", "z0", FAR, "yl")]
    rows, first, places = lax.optimization_barrier((stream, first, places))
    core = places[0]
    far = spread(rows, FAR, FARS)
    x_blocks = spread(far, NEAR, NEARS)
    part = on_core(
        logits_kernel,
        [((16, 144, 128), bf16)],
        x_blocks.reshape(NEARS, FARS * 16, 768),
        norm_gain,
        head_weight,
        flops=2 * 512 * 512 * 768,
    )[0]
    got = exchange(part, DEVICES)
    logits, scale, stats, mark = on_core(
        stats_kernel,
        [((32, 512), f32), ((32, 128), f32), ((32, 1, 128), f32), ((32, 512), f32)],
        first,
        got,
        targets,
        token_weight,
    )
    stats = exchange(stats, FAR + NEAR)
    sent = on_core(
        dlogits_kernel, [((8, 32, 1024), bf16)], stats, logits, scale, mark, gate_pre, up_pre
    )[0]
    mine = exchange(sent, CHIPS)
    others = other_core(mine)

    back = on_core(
        back_kernel,
        [((NEARS, FARS * 16, 768), bf16)],
        core,
        mine,
        others,
        head_weight,
        flops=2 * 512 * 512 * 768,
    )[0]
    near = jnp.sum(exchange(back, NEAR).astype(f32), axis=0).astype(bf16)
    got = exchange(near.reshape(FARS, 16, 768), FAR)
    sent = on_core(
        grad_kernel,
        [((FARS, 16, 768), bf16)],
        *places,
        got,
        mine,
        others,
        stream,
        norm_gain,
    )[0]
    gathered = spread(exchange(sent, FAR).reshape(FARS * 16, 768), NEAR, NEARS)
    hidden_part = hidden_back(gathered, down_weight)
    gathered, sent, x_blocks, mine, others, hidden_part = lax.optimization_barrier(
        (gathered, sent, x_blocks, mine, others, hidden_part)
    )
    stream_grad = sent[0]
    head_grad, down_grad, gain_grad = on_core(
        weights_kernel,
        [((512, 768), f32), ((448, 768), f32), ((1, 768), f32)],
        core,
        mine,
        others,
        x_blocks.reshape(NEARS, FARS * 16, 768),
        norm_gain,
        gathered,
        flops=2 * 512 * 960 * 768,
    )
    hidden_grad = jnp.sum(exchange(hidden_part.reshape(16, 32, 448), DEVICES).astype(f32), axis=0)
    gate_float = gate_pre.astype(f32)
    up_float = up_pre.astype(f32)
    sigmoid_gate = jax.nn.sigmoid(gate_float)
    up_grad = (hidden_grad * gate_float * sigmoid_gate).astype(bf16)
    gate_grad = (
        hidden_grad * up_float * sigmoid_gate * (1.0 + gate_float * (1.0 - sigmoid_gate))
    ).astype(bf16)
    return (head_grad, down_grad, stream_grad, gain_grad[0], gate_grad, up_grad)


def solution(mesh):
    fine = Mesh(mesh.devices.reshape((2,) * 9), TENSOR + DP)
    return jax.shard_map(
        per_device,
        mesh=fine,
        in_specs=(
            P(TENSOR, DP),
            P(DP),
            P(TENSOR, DP),
            P(TENSOR, DP),
            P(DP, TENSOR),
            P(DP, TENSOR),
            P(DP),
            P(DP),
        ),
        out_specs=(
            P(TENSOR, DP),
            P(TENSOR, DP),
            P(TENSOR, DP),
            P(DP),
            P(DP, TENSOR),
            P(DP, TENSOR),
        ),
        check_vma=False,
    )
```

```python
import jax
import jax.numpy as jnp
from jax import lax
from jax.experimental import pallas as pl
from jax.experimental.pallas import tpu as pltpu
from jax.sharding import Mesh, PartitionSpec as P

D = 12288
EPSILON = 1e-05
TENSOR = ("z3", "z2", "z1", "z0", "yl")
DP = ("yh", "x1", "x0", "c")
FAR, NEAR = ("z1", "z3", "z2"), ("z0", "yl")
CHIPS = ("x0", "yh", "x1")
DEVICES = CHIPS + ("c",)
FARS, NEARS = 8, 4
f32, bf16 = jnp.float32, jnp.bfloat16


def on_core(kernel, outs, *args, flops=0):
    whole = pl.BlockSpec(memory_space=pltpu.VMEM)
    outs = [jax.ShapeDtypeStruct(s, d) for s, d in outs]
    moved = sum(a.size * a.dtype.itemsize for a in list(args) + outs)
    return pl.pallas_call(
        kernel,
        out_shape=outs,
        in_specs=[
            pl.BlockSpec(memory_space=pltpu.SMEM) if a.shape == (1,) else whole for a in args
        ],
        out_specs=[whole] * len(outs),
        compiler_params=pltpu.CompilerParams(vmem_limit_bytes=16 << 20),
        cost_estimate=pl.CostEstimate(flops=flops, bytes_accessed=moved, transcendentals=0),
    )(*args)


def exchange(blocks, axes):
    return lax.all_to_all(blocks, axes, 0, 0, tiled=True)


def spread(block, axes, n):
    return exchange(jnp.broadcast_to(block[None], (n,) + block.shape), axes)


def other_core(block):
    return lax.ppermute(block, "c", [(0, 1), (1, 0)])


def token_rows(ref, first, count):
    return jnp.concatenate(
        [ref[n, f * 16 : f * 16 + 16] for f in range(first, first + count) for n in range(NEARS)]
    )


def columns_of(parts, width):
    lane = lax.broadcasted_iota(jnp.int32, (parts[0].shape[0], width), 1)
    out = jnp.zeros((parts[0].shape[0], width), f32)
    for k, part in enumerate(parts):
        out = jnp.where(lane == k, part, out)
    return out


def thirds(v):
    hi = v.astype(bf16).astype(f32)
    mid = (v - hi).astype(bf16).astype(f32)
    return [hi, mid, v - hi - mid]


def logits_kernel(x_ref, gain_ref, weight_ref, out_ref):
    gain = gain_ref[...].reshape(1, 768)
    for half in range(2):
        x = token_rows(x_ref, 4 * half, 4).astype(f32)
        scaled = (x * gain).astype(bf16)
        part = lax.dot_general(
            scaled, weight_ref[...], (((1,), (1,)), ((), ())), preferred_element_type=f32
        )
        part = part.astype(bf16)
        squares = jnp.sum(x * x, axis=1, keepdims=True)
        for k in range(8):
            to, rows = 8 * half + k, slice(32 * k, 32 * k + 32)
            for j in range(4):
                out_ref[to, 32 * j : 32 * j + 32, :] = part[rows, 128 * j : 128 * j + 128]
            row = row_of(thirds(squares[rows]))
            out_ref[to, 128:, :] = jnp.broadcast_to(row, (16, 128)).astype(bf16)


def row_of(columns):
    lane = lax.broadcasted_iota(jnp.int32, (32, 128), 1)
    token = lax.broadcasted_iota(jnp.int32, (32, 128), 0)
    spreaded = jnp.zeros((32, 128), f32)
    for k, column in enumerate(columns):
        spreaded = jnp.where(lane == token + 32 * k, column, spreaded)
    return jnp.sum(spreaded, axis=0, keepdims=True)


def column_of(row):
    lane = lax.broadcasted_iota(jnp.int32, (32, 128), 1)
    token = lax.broadcasted_iota(jnp.int32, (32, 128), 0)
    return jnp.sum(jnp.where(lane == token, row, 0.0), axis=1, keepdims=True)


def column(ref):
    row = ref[...].astype(f32).reshape(1, 32)
    lane = lax.broadcasted_iota(jnp.int32, (32, 32), 1)
    token = lax.broadcasted_iota(jnp.int32, (32, 32), 0)
    return jnp.sum(jnp.where(lane == token, row, 0.0), axis=1, keepdims=True)


def stats_kernel(
    first_ref, got_ref, targets_ref, weight_ref, logits_ref, scale_ref, stats_ref, mark_ref
):
    at = column(targets_ref).astype(jnp.int32) - first_ref[0]
    mark = (lax.broadcasted_iota(jnp.int32, (32, 512), 1) == at).astype(f32)
    total = jnp.zeros((144, 128), f32)
    for k in range(16):
        total = total + got_ref[k].astype(f32)
    lane = lax.broadcasted_iota(jnp.int32, (32, 128), 1)
    token = lax.broadcasted_iota(jnp.int32, (32, 128), 0)
    held = (lax.rem(lane, 32) == token) & (lane < 96)
    squares = jnp.sum(jnp.where(held, total[128:129], 0.0), axis=1, keepdims=True)
    inv = lax.rsqrt(squares / D + EPSILON)
    logits = jnp.concatenate([total[32 * j : 32 * j + 32] for j in range(4)], axis=1) * inv
    top = jnp.max(logits, axis=1, keepdims=True)
    e = jnp.exp(logits - top)
    row = row_of(
        [
            top,
            jnp.sum(e, axis=1, keepdims=True),
            jnp.sum(e * logits, axis=1, keepdims=True),
            jnp.sum(logits * mark, axis=1, keepdims=True),
        ]
    )
    logits_ref[...] = logits
    scale_ref[...] = columns_of([inv, column(weight_ref)], 128)
    mark_ref[...] = mark
    stats_ref[...] = jnp.broadcast_to(row[None], (32, 1, 128))


def dlogits_kernel(stats_ref, logits_ref, scale_ref, mark_ref, gate_ref, up_ref, out_ref):
    gate, up = gate_ref[...].astype(f32), up_ref[...].astype(f32)
    hidden = (gate * jax.nn.sigmoid(gate) * up).astype(bf16)
    stats = stats_ref[...].reshape(32, 128)
    lane = lax.broadcasted_iota(jnp.int32, (32, 128), 1)
    top = jnp.max(stats, axis=0, keepdims=True)
    scale = jnp.exp(jnp.where(lane < 32, stats - top, 0.0))
    sums = pltpu.roll(stats, 96, 1)
    means = pltpu.roll(stats, 64, 1)
    picked = pltpu.roll(stats, 32, 1)
    total = jnp.sum(sums * scale, axis=0, keepdims=True)
    mean = jnp.sum(means * scale, axis=0, keepdims=True) / total
    inner = mean - jnp.sum(picked, axis=0, keepdims=True)
    weight = scale_ref[:, 1:2]
    top, total, inner = column_of(top), column_of(total), column_of(inner) * weight / D
    probability = jnp.exp(logits_ref[...] - top) / total
    dlogits = ((probability - mark_ref[...]) * weight).astype(bf16)
    tail = columns_of(thirds(scale_ref[:, :1]) + thirds(inner), 64).astype(bf16)
    for k in range(8):
        out_ref[k, :, :512] = dlogits
        out_ref[k, :, 512:960] = hidden
        out_ref[k, :, 960:] = tail


def half_rows(core_ref, side, mine_ref, others_ref, lanes):
    here = core_ref[0] == side
    return jnp.concatenate(
        [
            jnp.where(here, mine_ref[f, y : y + 16, lanes], others_ref[f, y : y + 16, lanes])
            for y in (0, 16)
            for f in range(FARS)
        ]
    )


def back_kernel(core_ref, got_ref, weight_ref, *refs):
    out_ref = refs[-1]
    rows = [got_ref[f, y : y + 16, :512] for y in (0, 16) for f in range(FARS)]
    part = jnp.dot(jnp.concatenate(rows), weight_ref[...], preferred_element_type=f32)
    out_ref[2 * core_ref[0]] = part[:128].astype(bf16)
    out_ref[2 * core_ref[0] + 1] = part[128:].astype(bf16)


def back_half(core, got, weight, *into):
    whole = pl.BlockSpec(memory_space=pltpu.VMEM)
    return pl.pallas_call(
        back_kernel,
        out_shape=jax.ShapeDtypeStruct((NEARS, FARS * 16, 768), bf16),
        in_specs=[pl.BlockSpec(memory_space=pltpu.SMEM)] + [whole] * (2 + len(into)),
        out_specs=whole,
        input_output_aliases={3: 0} if into else {},
        compiler_params=pltpu.CompilerParams(vmem_limit_bytes=16 << 20),
        cost_estimate=pl.CostEstimate(
            flops=2 * 256 * 512 * 768, bytes_accessed=2 << 20, transcendentals=0
        ),
    )(core, got, weight, *into)


def weights_kernel(
    core_ref, mine_ref, others_ref, x_ref, gain_ref, rows_ref, head_ref, down_ref, sum_ref
):
    def add(ref, side, part):
        ref[...] = part if side == 0 else ref[...] + part

    def product(a, b):
        return lax.dot_general(a, b, (((0,), (0,)), ((), ())), preferred_element_type=f32)

    gain = gain_ref[...].reshape(1, 768)
    for side in range(2):
        got = half_rows(core_ref, side, mine_ref, others_ref, slice(0, 1024))
        tail = got[:, 896:].astype(f32)
        inv = tail[:, 64:65] + tail[:, 65:66] + tail[:, 66:67]
        inner = tail[:, 67:68] + tail[:, 68:69] + tail[:, 69:70]
        unit_rows = x_ref[2 * side : 2 * side + 2].reshape(256, 768).astype(f32) * inv
        add(head_ref, side, product(got[:, :512], (unit_rows * gain).astype(bf16)))
        rows = rows_ref[2 * side : 2 * side + 2].reshape(256, 768)
        add(down_ref, side, product(got[:, 512:960], rows))
        scaled = rows.astype(f32) * (1.0 / inv) + unit_rows * inner
        add(sum_ref, side, jnp.sum(scaled * unit_rows, axis=0, keepdims=True))
    sum_ref[...] = sum_ref[...] / gain


def grad_kernel(
    core_ref, near_ref, far_ref, low_ref, got_ref, mine_ref, others_ref, x_ref, gain_ref,
    out_ref,
):
    rows = pl.ds(pl.multiple_of(low_ref[0] * 16, 16), 16)
    here = core_ref[0] == near_ref[0]
    tail = jnp.where(
        here, mine_ref[far_ref[0], rows, 896:], others_ref[far_ref[0], rows, 896:]
    ).astype(f32)
    inv = tail[:, 64:65] + tail[:, 65:66] + tail[:, 66:67]
    inner = tail[:, 67:68] + tail[:, 68:69] + tail[:, 69:70]
    normed_back = jnp.zeros((16, 768), f32)
    for k in range(FARS):
        normed_back = normed_back + got_ref[k].astype(f32)
    unit_rows = x_ref[...].astype(f32) * inv
    grad = (inv * (normed_back * gain_ref[...].reshape(1, 768) - unit_rows * inner)).astype(bf16)
    for k in range(FARS):
        out_ref[k] = grad


def hidden_back_kernel(rows_ref, weight_ref, out_ref, held, sems):
    copies = []
    for half in range(2):
        rows = pl.ds(256 * half, 256)
        part = lax.dot_general(
            token_rows(rows_ref, 4 * half, 4),
            weight_ref[...],
            (((1,), (1,)), ((), ())),
            preferred_element_type=f32,
        )
        held[rows, :] = part.astype(bf16)
        copies.append(pltpu.make_async_copy(held.at[rows], out_ref.at[rows], sems.at[half]))
        copies[-1].start()
    for copy in copies:
        copy.wait()


def hidden_back(rows, weight):
    shape, whole = (512, 448), pl.BlockSpec(memory_space=pltpu.VMEM)
    return pl.pallas_call(
        hidden_back_kernel,
        out_shape=jax.ShapeDtypeStruct(shape, bf16),
        in_specs=[whole, whole],
        out_specs=pl.BlockSpec(memory_space=pl.ANY),
        scratch_shapes=[pltpu.VMEM(shape, bf16), pltpu.SemaphoreType.DMA((2,))],
        compiler_params=pltpu.CompilerParams(vmem_limit_bytes=16 << 20),
        cost_estimate=pl.CostEstimate(
            flops=2 * 512 * 448 * 768, bytes_accessed=2 << 20, transcendentals=0
        ),
    )(rows, weight)


def per_device(
    stream, norm_gain, head_weight, down_weight, gate_pre, up_pre, targets, token_weight
):
    vocab_local = head_weight.shape[0]
    t = lax.axis_index(TENSOR)
    first = (t * vocab_local).astype(jnp.int32)[None]
    places = [lax.axis_index(a).astype(jnp.int32)[None] for a in ("c", "z0", FAR, "yl")]
    rows, first, places, twin = lax.optimization_barrier((stream, first, places, 1 - places[0]))
    core = places[0]
    far = spread(rows, FAR, FARS)
    x_blocks = spread(far, NEAR, NEARS)
    part = on_core(
        logits_kernel,
        [((16, 144, 128), bf16)],
        x_blocks.reshape(NEARS, FARS * 16, 768),
        norm_gain,
        head_weight,
        flops=2 * 512 * 512 * 768,
    )[0]
    got = exchange(part, DEVICES)
    logits, scale, stats, mark = on_core(
        stats_kernel,
        [((32, 512), f32), ((32, 128), f32), ((32, 1, 128), f32), ((32, 512), f32)],
        first,
        got,
        targets,
        token_weight,
    )
    stats = exchange(stats, FAR + NEAR)
    sent = on_core(
        dlogits_kernel, [((8, 32, 1024), bf16)], stats, logits, scale, mark, gate_pre, up_pre
    )[0]
    mine = exchange(sent, CHIPS)
    others = other_core(mine)

    back = back_half(core, mine, head_weight)
    back = back_half(twin, others, head_weight, back)
    near = jnp.sum(exchange(back, NEAR).astype(f32), axis=0).astype(bf16)
    got = exchange(near.reshape(FARS, 16, 768), FAR)
    sent = on_core(
        grad_kernel,
        [((FARS, 16, 768), bf16)],
        *places,
        got,
        mine,
        others,
        stream,
        norm_gain,
    )[0]
    gathered = spread(exchange(sent, FAR).reshape(FARS * 16, 768), NEAR, NEARS)
    hidden_part = hidden_back(gathered, down_weight)
    gathered, sent, x_blocks, mine, others, hidden_part = lax.optimization_barrier(
        (gathered, sent, x_blocks, mine, others, hidden_part)
    )
    stream_grad = sent[0]
    head_grad, down_grad, gain_grad = on_core(
        weights_kernel,
        [((512, 768), f32), ((448, 768), f32), ((1, 768), f32)],
        core,
        mine,
        others,
        x_blocks.reshape(NEARS, FARS * 16, 768),
        norm_gain,
        gathered,
        flops=2 * 512 * 960 * 768,
    )
    hidden_grad = jnp.sum(exchange(hidden_part.reshape(16, 32, 448), DEVICES).astype(f32), axis=0)
    gate_float = gate_pre.astype(f32)
    up_float = up_pre.astype(f32)
    sigmoid_gate = jax.nn.sigmoid(gate_float)
    up_grad = (hidden_grad * gate_float * sigmoid_gate).astype(bf16)
    gate_grad = (
        hidden_grad * up_float * sigmoid_gate * (1.0 + gate_float * (1.0 - sigmoid_gate))
    ).astype(bf16)
    return (head_grad, down_grad, stream_grad, gain_grad[0], gate_grad, up_grad)


def solution(mesh):
    fine = Mesh(mesh.devices.reshape((2,) * 9), TENSOR + DP)
    return jax.shard_map(
        per_device,
        mesh=fine,
        in_specs=(
            P(TENSOR, DP),
            P(DP),
            P(TENSOR, DP),
            P(TENSOR, DP),
            P(DP, TENSOR),
            P(DP, TENSOR),
            P(DP),
            P(DP),
        ),
        out_specs=(
            P(TENSOR, DP),
            P(TENSOR, DP),
            P(TENSOR, DP),
            P(DP),
            P(DP, TENSOR),
            P(DP, TENSOR),
        ),
        check_vma=False,
    )
```

```python
import jax
import jax.numpy as jnp
from jax import lax
from jax.experimental import pallas as pl
from jax.experimental.pallas import tpu as pltpu
from jax.sharding import Mesh, PartitionSpec as P

D = 12288
EPSILON = 1e-05
TENSOR = ("z3", "z2", "z1", "z0", "yl")
DP = ("yh", "x1", "x0", "c")
FAR, NEAR = ("z1", "z2", "z3"), ("z0", "yl")
CHIPS = ("x0", "x1", "yh")
DEVICES = CHIPS + ("c",)
FARS, NEARS = 8, 4
f32, bf16 = jnp.float32, jnp.bfloat16


def on_core(kernel, outs, *args, flops=0):
    whole = pl.BlockSpec(memory_space=pltpu.VMEM)
    outs = [jax.ShapeDtypeStruct(s, d) for s, d in outs]
    moved = sum(a.size * a.dtype.itemsize for a in list(args) + outs)
    return pl.pallas_call(
        kernel,
        out_shape=outs,
        in_specs=[
            pl.BlockSpec(memory_space=pltpu.SMEM) if a.shape == (1,) else whole for a in args
        ],
        out_specs=[whole] * len(outs),
        compiler_params=pltpu.CompilerParams(vmem_limit_bytes=16 << 20),
        cost_estimate=pl.CostEstimate(flops=flops, bytes_accessed=moved, transcendentals=0),
    )(*args)


def exchange(blocks, axes):
    return lax.all_to_all(blocks, axes, 0, 0, tiled=True)


def spread(block, axes, n):
    return exchange(jnp.broadcast_to(block[None], (n,) + block.shape), axes)


def other_core(block):
    return lax.ppermute(block, "c", [(0, 1), (1, 0)])


def token_rows(ref, first, count):
    return jnp.concatenate(
        [ref[n, f * 16 : f * 16 + 16] for f in range(first, first + count) for n in range(NEARS)]
    )


def columns_of(parts, width):
    lane = lax.broadcasted_iota(jnp.int32, (parts[0].shape[0], width), 1)
    out = jnp.zeros((parts[0].shape[0], width), f32)
    for k, part in enumerate(parts):
        out = jnp.where(lane == k, part, out)
    return out


def thirds(v):
    hi = v.astype(bf16).astype(f32)
    mid = (v - hi).astype(bf16).astype(f32)
    return [hi, mid, v - hi - mid]


def logits_kernel(x_ref, gain_ref, weight_ref, out_ref):
    gain = gain_ref[...].reshape(1, 768)
    for half in range(2):
        x = token_rows(x_ref, 4 * half, 4).astype(f32)
        scaled = (x * gain).astype(bf16)
        part = lax.dot_general(
            scaled, weight_ref[...], (((1,), (1,)), ((), ())), preferred_element_type=f32
        )
        part = part.astype(bf16)
        squares = jnp.sum(x * x, axis=1, keepdims=True)
        for k in range(8):
            to, rows = 8 * half + k, slice(32 * k, 32 * k + 32)
            for j in range(4):
                out_ref[to, 32 * j : 32 * j + 32, :] = part[rows, 128 * j : 128 * j + 128]
            row = row_of(thirds(squares[rows]))
            out_ref[to, 128:, :] = jnp.broadcast_to(row, (16, 128)).astype(bf16)


def row_of(columns):
    lane = lax.broadcasted_iota(jnp.int32, (32, 128), 1)
    token = lax.broadcasted_iota(jnp.int32, (32, 128), 0)
    spreaded = jnp.zeros((32, 128), f32)
    for k, column in enumerate(columns):
        spreaded = jnp.where(lane == token + 32 * k, column, spreaded)
    return jnp.sum(spreaded, axis=0, keepdims=True)


def column_of(row):
    lane = lax.broadcasted_iota(jnp.int32, (32, 128), 1)
    token = lax.broadcasted_iota(jnp.int32, (32, 128), 0)
    return jnp.sum(jnp.where(lane == token, row, 0.0), axis=1, keepdims=True)


def column(ref):
    row = ref[...].astype(f32).reshape(1, 32)
    lane = lax.broadcasted_iota(jnp.int32, (32, 32), 1)
    token = lax.broadcasted_iota(jnp.int32, (32, 32), 0)
    return jnp.sum(jnp.where(lane == token, row, 0.0), axis=1, keepdims=True)


def stats_kernel(
    first_ref, got_ref, targets_ref, weight_ref, logits_ref, scale_ref, stats_ref, mark_ref
):
    at = column(targets_ref).astype(jnp.int32) - first_ref[0]
    mark = (lax.broadcasted_iota(jnp.int32, (32, 512), 1) == at).astype(f32)
    total = jnp.zeros((144, 128), f32)
    for k in range(16):
        total = total + got_ref[k].astype(f32)
    lane = lax.broadcasted_iota(jnp.int32, (32, 128), 1)
    token = lax.broadcasted_iota(jnp.int32, (32, 128), 0)
    held = (lax.rem(lane, 32) == token) & (lane < 96)
    squares = jnp.sum(jnp.where(held, total[128:129], 0.0), axis=1, keepdims=True)
    inv = lax.rsqrt(squares / D + EPSILON)
    logits = jnp.concatenate([total[32 * j : 32 * j + 32] for j in range(4)], axis=1) * inv
    top = jnp.max(logits, axis=1, keepdims=True)
    e = jnp.exp(logits - top)
    row = row_of(
        [
            top,
            jnp.sum(e, axis=1, keepdims=True),
            jnp.sum(e * logits, axis=1, keepdims=True),
            jnp.sum(logits * mark, axis=1, keepdims=True),
        ]
    )
    logits_ref[...] = logits
    scale_ref[...] = columns_of([inv, column(weight_ref)], 128)
    mark_ref[...] = mark
    stats_ref[...] = jnp.broadcast_to(row[None], (32, 1, 128))


def dlogits_kernel(stats_ref, logits_ref, scale_ref, mark_ref, gate_ref, up_ref, out_ref):
    gate, up = gate_ref[...].astype(f32), up_ref[...].astype(f32)
    hidden = (gate * jax.nn.sigmoid(gate) * up).astype(bf16)
    stats = stats_ref[...].reshape(32, 128)
    lane = lax.broadcasted_iota(jnp.int32, (32, 128), 1)
    top = jnp.max(stats, axis=0, keepdims=True)
    scale = jnp.exp(jnp.where(lane < 32, stats - top, 0.0))
    sums = pltpu.roll(stats, 96, 1)
    means = pltpu.roll(stats, 64, 1)
    picked = pltpu.roll(stats, 32, 1)
    total = jnp.sum(sums * scale, axis=0, keepdims=True)
    mean = jnp.sum(means * scale, axis=0, keepdims=True) / total
    inner = mean - jnp.sum(picked, axis=0, keepdims=True)
    weight = scale_ref[:, 1:2]
    top, total, inner = column_of(top), column_of(total), column_of(inner) * weight / D
    probability = jnp.exp(logits_ref[...] - top) / total
    dlogits = ((probability - mark_ref[...]) * weight).astype(bf16)
    tail = columns_of(thirds(scale_ref[:, :1]) + thirds(inner), 64).astype(bf16)
    for k in range(8):
        out_ref[k, :, :512] = dlogits
        out_ref[k, :, 512:960] = hidden
        out_ref[k, :, 960:] = tail


def half_rows(core_ref, side, mine_ref, others_ref, lanes):
    here = core_ref[0] == side
    return jnp.concatenate(
        [
            jnp.where(here, mine_ref[f, y : y + 16, lanes], others_ref[f, y : y + 16, lanes])
            for y in (0, 16)
            for f in range(FARS)
        ]
    )


def back_kernel(core_ref, mine_ref, others_ref, weight_ref, out_ref):
    for side in range(2):
        rows = half_rows(core_ref, side, mine_ref, others_ref, slice(0, 512))
        part = jnp.dot(rows, weight_ref[...], preferred_element_type=f32)
        out_ref[2 * side] = part[:128].astype(bf16)
        out_ref[2 * side + 1] = part[128:].astype(bf16)


def weights_kernel(
    core_ref, mine_ref, others_ref, x_ref, gain_ref, rows_ref, head_ref, down_ref, sum_ref
):
    def add(ref, side, part):
        ref[...] = part if side == 0 else ref[...] + part

    def product(a, b):
        return lax.dot_general(a, b, (((0,), (0,)), ((), ())), preferred_element_type=f32)

    gain = gain_ref[...].reshape(1, 768)
    for side in range(2):
        got = half_rows(core_ref, side, mine_ref, others_ref, slice(0, 1024))
        tail = got[:, 896:].astype(f32)
        inv = tail[:, 64:65] + tail[:, 65:66] + tail[:, 66:67]
        inner = tail[:, 67:68] + tail[:, 68:69] + tail[:, 69:70]
        unit_rows = x_ref[2 * side : 2 * side + 2].reshape(256, 768).astype(f32) * inv
        add(head_ref, side, product(got[:, :512], (unit_rows * gain).astype(bf16)))
        rows = rows_ref[2 * side : 2 * side + 2].reshape(256, 768)
        add(down_ref, side, product(got[:, 512:960], rows))
        scaled = rows.astype(f32) * (1.0 / inv) + unit_rows * inner
        add(sum_ref, side, jnp.sum(scaled * unit_rows, axis=0, keepdims=True))
    sum_ref[...] = sum_ref[...] / gain


def grad_kernel(
    core_ref, near_ref, far_ref, low_ref, got_ref, mine_ref, others_ref, x_ref, gain_ref,
    out_ref,
):
    rows = pl.ds(pl.multiple_of(low_ref[0] * 16, 16), 16)
    here = core_ref[0] == near_ref[0]
    tail = jnp.where(
        here, mine_ref[far_ref[0], rows, 896:], others_ref[far_ref[0], rows, 896:]
    ).astype(f32)
    inv = tail[:, 64:65] + tail[:, 65:66] + tail[:, 66:67]
    inner = tail[:, 67:68] + tail[:, 68:69] + tail[:, 69:70]
    normed_back = jnp.zeros((16, 768), f32)
    for k in range(FARS):
        normed_back = normed_back + got_ref[k].astype(f32)
    unit_rows = x_ref[...].astype(f32) * inv
    grad = (inv * (normed_back * gain_ref[...].reshape(1, 768) - unit_rows * inner)).astype(bf16)
    for k in range(FARS):
        out_ref[k] = grad


def hidden_back_kernel(rows_ref, weight_ref, out_ref, held, sems):
    copies = []
    for half in range(2):
        rows = pl.ds(256 * half, 256)
        part = lax.dot_general(
            token_rows(rows_ref, 4 * half, 4),
            weight_ref[...],
            (((1,), (1,)), ((), ())),
            preferred_element_type=f32,
        )
        held[rows, :] = part.astype(bf16)
        copies.append(pltpu.make_async_copy(held.at[rows], out_ref.at[rows], sems.at[half]))
        copies[-1].start()
    for copy in copies:
        copy.wait()


def hidden_back(rows, weight):
    shape, whole = (512, 448), pl.BlockSpec(memory_space=pltpu.VMEM)
    return pl.pallas_call(
        hidden_back_kernel,
        out_shape=jax.ShapeDtypeStruct(shape, bf16),
        in_specs=[whole, whole],
        out_specs=pl.BlockSpec(memory_space=pl.ANY),
        scratch_shapes=[pltpu.VMEM(shape, bf16), pltpu.SemaphoreType.DMA((2,))],
        compiler_params=pltpu.CompilerParams(vmem_limit_bytes=16 << 20),
        cost_estimate=pl.CostEstimate(
            flops=2 * 512 * 448 * 768, bytes_accessed=2 << 20, transcendentals=0
        ),
    )(rows, weight)


def per_device(
    stream, norm_gain, head_weight, down_weight, gate_pre, up_pre, targets, token_weight
):
    vocab_local = head_weight.shape[0]
    t = lax.axis_index(TENSOR)
    first = (t * vocab_local).astype(jnp.int32)[None]
    places = [lax.axis_index(a).astype(jnp.int32)[None] for a in ("c", "z0", FAR, "yl")]
    rows, first, places = lax.optimization_barrier((stream, first, places))
    core = places[0]
    far = spread(rows, FAR, FARS)
    x_blocks = spread(far, NEAR, NEARS)
    part = on_core(
        logits_kernel,
        [((16, 144, 128), bf16)],
        x_blocks.reshape(NEARS, FARS * 16, 768),
        norm_gain,
        head_weight,
        flops=2 * 512 * 512 * 768,
    )[0]
    got = exchange(part, DEVICES)
    logits, scale, stats, mark = on_core(
        stats_kernel,
        [((32, 512), f32), ((32, 128), f32), ((32, 1, 128), f32), ((32, 512), f32)],
        first,
        got,
        targets,
        token_weight,
    )
    stats = exchange(stats, FAR + NEAR)
    sent = on_core(
        dlogits_kernel, [((8, 32, 1024), bf16)], stats, logits, scale, mark, gate_pre, up_pre
    )[0]
    mine = exchange(sent, CHIPS)
    others = other_core(mine)

    back = on_core(
        back_kernel,
        [((NEARS, FARS * 16, 768), bf16)],
        core,
        mine,
        others,
        head_weight,
        flops=2 * 512 * 512 * 768,
    )[0]
    near = jnp.sum(exchange(back, NEAR).astype(f32), axis=0).astype(bf16)
    got = exchange(near.reshape(FARS, 16, 768), FAR)
    sent = on_core(
        grad_kernel,
        [((FARS, 16, 768), bf16)],
        *places,
        got,
        mine,
        others,
        stream,
        norm_gain,
    )[0]
    gathered = spread(exchange(sent, FAR).reshape(FARS * 16, 768), NEAR, NEARS)
    hidden_part = hidden_back(gathered, down_weight)
    gathered, sent, x_blocks, mine, others, hidden_part = lax.optimization_barrier(
        (gathered, sent, x_blocks, mine, others, hidden_part)
    )
    stream_grad = sent[0]
    head_grad, down_grad, gain_grad = on_core(
        weights_kernel,
        [((512, 768), f32), ((448, 768), f32), ((1, 768), f32)],
        core,
        mine,
        others,
        x_blocks.reshape(NEARS, FARS * 16, 768),
        norm_gain,
        gathered,
        flops=2 * 512 * 960 * 768,
    )
    hidden_grad = jnp.sum(exchange(hidden_part.reshape(16, 32, 448), DEVICES).astype(f32), axis=0)
    gate_float = gate_pre.astype(f32)
    up_float = up_pre.astype(f32)
    sigmoid_gate = jax.nn.sigmoid(gate_float)
    up_grad = (hidden_grad * gate_float * sigmoid_gate).astype(bf16)
    gate_grad = (
        hidden_grad * up_float * sigmoid_gate * (1.0 + gate_float * (1.0 - sigmoid_gate))
    ).astype(bf16)
    return (head_grad, down_grad, stream_grad, gain_grad[0], gate_grad, up_grad)


def solution(mesh):
    fine = Mesh(mesh.devices.reshape((2,) * 9), TENSOR + DP)
    return jax.shard_map(
        per_device,
        mesh=fine,
        in_specs=(
            P(TENSOR, DP),
            P(DP),
            P(TENSOR, DP),
            P(TENSOR, DP),
            P(DP, TENSOR),
            P(DP, TENSOR),
            P(DP),
            P(DP),
        ),
        out_specs=(
            P(TENSOR, DP),
            P(TENSOR, DP),
            P(TENSOR, DP),
            P(DP),
            P(DP, TENSOR),
            P(DP, TENSOR),
        ),
        check_vma=False,
    )
```
